256 devices in a mesh: dp: 4 (over x), vocab: 64 (over y, z, core).
Axes of the slice: x: 4, y: 4, z: 8, core: 2. Of those that a mesh axis runs over, the one named last changes fastest.
Arguments:
- features: bfloat16 [2048, 4096], P(('dp', 'vocab')), may hold values from -8 to 8
- head: bfloat16 [65536, 4096], P(('dp', 'vocab')), may hold values from -0.5 to 0.5
- momentum: bfloat16 [65536, 4096], P(('dp', 'vocab')), may hold values from -7.124618e-08 to 7.124618e-08
- hessian: bfloat16 [65536, 4096], P(('dp', 'vocab')), may hold values from 4.765752e-10 to 4.7683716e-06
- true_labels: int32 [2048], replicated, may hold values from 0 to 65535
- sampled_labels: int32 [2048], replicated, may hold values from 0 to 65535
Outputs:
- mean_loss: float32 [], replicated
- new_hessian: bfloat16 [65536, 4096], P(('dp', 'vocab'))
- update: bfloat16 [65536, 4096], P(('dp', 'vocab'))
The draws below stay inside these ranges and needn't reach their ends.
All inputs are finite; a program needn't handle non-finite values.
Results may differ from the reference program's by a relative error of at most 0.019.
Values may be sent and summed in bfloat16 or wider, within the bound.
A program may use at most 128 MiB of HBM per device.

```python
import math
import jax
import jax.numpy as jnp
import numpy as np
from jax import lax

D = 4096
TOK_DEV = 512
TOKENS = 2048
VOCAB = 65536
N_DP = 4


def head_rows(key, wanted):
    row_key = jax.random.fold_in(key, 11)

    def single(index):
        return jax.random.normal(jax.random.fold_in(row_key, index), (D,), jnp.float32)
    return jax.vmap(single)(wanted) * (3.0 / math.sqrt(D))


def draw_head(key, part):
    every_row = head_rows(key, jnp.arange(VOCAB, dtype=jnp.int32))
    return jnp.clip(every_row, -0.5, 0.5).astype(jnp.bfloat16)


def draw_features(key, part):
    own_key = jax.random.fold_in(key, 5)
    values = jax.random.normal(own_key, (TOKENS, D), jnp.float32)
    return jnp.clip(values, -8.0, 8.0).astype(jnp.bfloat16)


def set_ends(drawn, stream_key, low, largest):
    longest = drawn.shape.index(max(drawn.shape))
    spots = []
    for shift in (0, 1):
        where = [jax.random.randint(jax.random.fold_in(stream_key, axis), (), 0, length) for axis, length in enumerate(drawn.shape)]
        where[longest] = (where[longest] + shift) % drawn.shape[longest]
        spots.append(tuple(where))
    return drawn.at[spots[0]].set(low).at[spots[1]].set(largest)


def level_of(rng, shape, shards, least, largest):
    def one(position, parts):
        draws = jax.random.uniform(jax.random.fold_in(jax.random.fold_in(rng, 6), position), (parts,), jnp.float32, least / len(shards), largest / len(shards))
        return jnp.repeat(jnp.exp(draws), shape[position] // parts).reshape((-1,) + (1,) * (len(shape) - position - 1))

    loudness = one(*shards[0])
    for cut in shards[1:]:
        loudness = loudness * one(*cut)
    return loudness


def cumulative_ranks(number_of, lean):
    portions = [(1 << 20) // math.isqrt(grade ** lean) + 1 for grade in range(1, number_of + 1)]
    scale = 1 + sum(portions) // (1 << 30)
    return np.cumsum(np.array([max(1, weight // scale) for weight in portions]))


def skewed_ids(rng, extent, count, skew):
    grid = cumulative_ranks(count, skew)
    ticket = jax.random.randint(jax.random.fold_in(rng, 1), extent, 0, int(grid[count - 1]))
    grade = jnp.searchsorted(jnp.asarray(grid, jnp.int32), ticket, side="right")
    return jax.random.permutation(jax.random.fold_in(rng, 2), count)[grade].astype(jnp.int32)


def centred(stream_key, extent, spread, limit, shards=(), held_as=jnp.bfloat16):
    entries = jax.random.normal(stream_key, extent, jnp.float32) * spread
    if len(shards) > 0:
        entries = level_of(stream_key, extent, shards, -0.22, 0.18) * entries
    return jnp.clip(entries, min=-limit, max=limit).astype(held_as)


def setup_inputs(seed: int = 0) -> dict:
    key_of = jax.random.split(jax.random.key(seed), 7)
    features = draw_features(jax.random.fold_in(key_of[6], 71), 0)
    head = draw_head(jax.random.fold_in(key_of[6], 71), 0)
    momentum = centred(key_of[2], (VOCAB, D), (0.025 * TOKENS * VOCAB ** -2), 7.12461769580841e-08, ((0, 256),))
    hessian = jnp.clip(jnp.exp(math.log(4.76837158203125e-06) - 9.21089 * jax.random.uniform(key_of[3], (VOCAB, D), jnp.float32) ** level_of(key_of[3], (VOCAB, D), ((0, 256),), -0.2, 0.2)), 4.765752237290144e-10, 4.76837158203125e-06).astype(jnp.bfloat16)
    true_labels = set_ends(skewed_ids(key_of[4], (TOKENS,), VOCAB, 2), jax.random.fold_in(key_of[4], 3), 0, VOCAB - 1).astype(jnp.int32)
    sampled_labels = set_ends(skewed_ids(key_of[5], (TOKENS,), VOCAB, 1), jax.random.fold_in(key_of[5], 3), 0, VOCAB - 1).astype(jnp.int32)
    return dict(features=features, head=head, momentum=momentum, hessian=hessian, true_labels=true_labels, sampled_labels=sampled_labels)


hess_decay = 0.99
clip_scale = 0.05


def reference(features, head, momentum, hessian, true_labels, sampled_labels):
    logits = lax.dot_general(features, head, (((1,), (1,)), ((), ())), preferred_element_type=jnp.float32)
    log_norm = jax.nn.logsumexp(logits, axis=1)
    picked = jnp.take_along_axis(logits, true_labels[:, None].astype(jnp.int32), axis=1)[:, 0]
    mean_loss = jnp.mean(log_norm - picked)
    columns = jnp.arange(VOCAB, dtype=jnp.int32)
    chosen = (columns[None, :] == sampled_labels[:, None]).astype(jnp.float32)
    signal = (jnp.exp(logits - log_norm[:, None]) - chosen).astype(jnp.bfloat16)

    def add_group(total, index):
        start = (index * TOK_DEV).astype(jnp.int32)
        rows = lax.dynamic_slice_in_dim(signal, start, TOK_DEV, 0)
        group_rows = lax.dynamic_slice_in_dim(features, start, TOK_DEV, 0)
        partial_sum = lax.dot_general(rows, group_rows, (((0,), (0,)), ((), ())), preferred_element_type=jnp.float32)
        rounded = lax.optimization_barrier(partial_sum.astype(jnp.bfloat16)).astype(jnp.float32)
        return total + rounded, None

    gradient, _ = lax.scan(add_group, jnp.zeros((VOCAB, D), jnp.float32), jnp.arange(N_DP, dtype=jnp.int32))
    fresh = hess_decay * hessian.astype(jnp.float32) + (1.0 - hess_decay) * gradient * gradient
    clipped = jnp.clip(momentum.astype(jnp.float32) / (clip_scale * fresh), -1.0, 1.0)
    return mean_loss, fresh.astype(jnp.bfloat16), clipped.astype(jnp.bfloat16)
```

```python
import jax
import jax.numpy as jnp
from jax import lax
from jax.experimental import pallas as pl
from jax.experimental.pallas import tpu as pltpu
from jax.sharding import PartitionSpec as P

MESH = pl.DeviceIdType.MESH
hess_decay = 0.99
clip_scale = 0.05

NX, NY, NZ = 4, 4, 8
D = 4096
HALF = D // 2
ROWS = 16
BLOCK = 256
TOKENS = 2048
VOC = 256
STAT = 384


def gather_kernel(feat_ref, head_ref, true_ref, samp_ref,
                  feats_out, signal_ref, loss_ref,
                  pair, held, logits, stats_a, stats_b,
                  pair_s, pair_r, q_s, q_r, z_s, z_r, zh_s, zh_r,
                  p_s, p_r, s_s, s_r, a_s, a_r, b_s, b_r, out_sem):
    x = lax.axis_index("dp")
    v = lax.axis_index("vocab")
    y, z, c = v // 16, (v // 2) % 8, v % 2
    p = jnp.where(c == 0, x, y)
    q = jnp.where(c == 0, y, x)

    def device(px, qx, zx):
        xx = jnp.where(c == 0, px, qx)
        yy = jnp.where(c == 0, qx, px)
        return (xx, yy * 16 + zx * 2 + c)

    sister = (x, y * 16 + z * 2 + 1 - c)
    p_up, p_dn = (p + 1) % 4, (p + 3) % 4
    q_up, q_dn = (q + 1) % 4, (q + 3) % 4
    z_up, z_dn = (z + 1) % 8, (z + 7) % 8

    def remote(src, dst, ssem, rsem, dev):
        return pltpu.make_async_remote_copy(src, dst, ssem, rsem, device_id=dev, device_id_type=MESH)

    barrier = pltpu.get_barrier_semaphore()
    for dev in (sister, device(p_up, q, z), device(p_dn, q, z), device(p, q_up, z), device(p, q_dn, z),
                device(p, q, z_up), device(p, q, z_dn)):
        pl.semaphore_signal(barrier, inc=1, device_id=dev, device_id_type=MESH)
    pl.semaphore_wait(barrier, 7)

    theirs = pl.multiple_of((1 - c) * HALF, HALF)
    mine = pl.multiple_of(c * HALF, HALF)
    pair_copy = remote(feat_ref.at[:, pl.ds(theirs, HALF)], pair.at[c], pair_s, pair_r, sister)
    pair_copy.start()
    pair[c] = feat_ref[:, pl.ds(mine, HALF)]
    pair_copy.wait_recv()
    held[c, z, p, q] = pair[...].reshape(ROWS, HALF)

    def slab(qx):
        return held.at[c, z, p, qx]

    q_copies = [
        remote(slab(q), slab(q), q_s.at[0], q_r.at[0], device(p, q_up, z)),
        remote(slab(q), slab(q), q_s.at[1], q_r.at[1], device(p, q_dn, z)),
        remote(slab(q_dn), slab(q_dn), q_s.at[2], q_r.at[2], device(p, q_up, z)),
    ]
    q_copies[0].start()
    q_copies[1].start()
    q_copies[0].wait_recv()
    q_copies[2].start()
    q_copies[1].wait_recv()
    q_copies[2].wait_recv()

    def plane(s):
        off = jnp.where(s % 2 == 1, 8 - (s + 1) // 2, s // 2)
        return (z + off) % 8

    def chunk(zx, px):
        return held.at[c, zx, px]

    def part(zx, px, half):
        return held.at[c, zx, px, pl.ds(half * 2, 2)]

    def z_copy(s):
        zx = plane(s)
        to = jnp.where(s % 2 == 1, z_up, z_dn)
        return remote(chunk(zx, p), chunk(zx, p), z_s.at[s + 2], z_r.at[s + 2], device(p, q, to))

    def z_half(s):
        zx = plane(s)
        to = jnp.where(s % 2 == 1, z_up, z_dn)
        return remote(part(zx, p, s - 5), part(zx, p, s - 5), zh_s.at[s - 5], zh_r.at[s - 5], device(p, q, to))

    def z_first():
        return remote(chunk(z, p), chunk(z, p), z_s.at[1], z_r.at[1], device(p, q, z_up))

    def p_copies(s):
        zx = plane(s)
        return (remote(chunk(zx, p), chunk(zx, p), p_s.at[s, 0], p_r.at[s, 0], device(p_up, q, z)),
                remote(chunk(zx, p), chunk(zx, p), p_s.at[s, 1], p_r.at[s, 1], device(p_dn, q, z)))

    def p_halves(s):
        zx = plane(s)
        return (remote(part(zx, p_dn, 0), part(zx, p_dn, 0), p_s.at[s, 2], p_r.at[s, 2], device(p_up, q, z)),
                remote(part(zx, p_up, 1), part(zx, p_up, 1), p_s.at[s, 3], p_r.at[s, 3], device(p_dn, q, z)))

    def s_copy(s, which, px):
        zx = plane(s)
        return remote(chunk(zx, px), chunk(zx, px), s_s.at[s, which], s_r.at[s, which], sister)

    p_far = (p + 2) % 4

    def spread(s):
        for copy in p_copies(s):
            copy.start()
        s_copy(s, 0, p).start()

    z_first().start()
    z_copy(0).start()
    spread(0)

    own_offset = (x * 64 + v) * VOC
    rows = own_offset + lax.broadcasted_iota(jnp.int32, (VOC, BLOCK), 0)
    lanes = lax.broadcasted_iota(jnp.int32, (1, STAT), 1)
    planes = lax.broadcasted_iota(jnp.int32, (NZ, STAT), 0)
    stats_a[x * 4 + y] = jnp.zeros((NZ, STAT), jnp.float32)

    def out_copies(s):
        zx = plane(s)
        copies = [pltpu.make_async_copy(held.at[0, zx], feats_out.at[zx, :, :, :, pl.ds(0, HALF)], out_sem.at[s, 0])]
        for yy in range(NY):
            copies.append(pltpu.make_async_copy(
                held.at[1, zx, yy], feats_out.at[zx, :, yy, :, pl.ds(HALF, HALF)], out_sem.at[s, 1 + yy]))
        return copies

    def compute(s):
        zx = plane(s)
        left = held[0, zx].reshape(BLOCK, HALF)
        total = lax.dot_general(head_ref[:, :HALF], left, (((1,), (1,)), ((), ())), preferred_element_type=jnp.float32)
        right = jnp.concatenate([held[1, zx, yy, xx] for xx in range(NX) for yy in range(NY)], axis=0)
        total += lax.dot_general(head_ref[:, HALF:], right, (((1,), (1,)), ((), ())), preferred_element_type=jnp.float32)
        logits[zx] = total
        highest = jnp.max(total, axis=0, keepdims=True)
        lse = highest + jnp.log(jnp.sum(jnp.exp(total - highest), axis=0, keepdims=True))
        labels = true_ref[pl.ds(zx, 1), :]
        picked = jnp.sum(jnp.where(rows == labels, total, 0.0), axis=0, keepdims=True)
        return zx, lse, picked

    me_xy = x * 4 + y
    me_zc = z * 2 + c

    def step(i, carry):
        @pl.when(jnp.logical_and(i >= 1, i <= 6))
        def _():
            z_copy(i - 2).wait_recv()

        @pl.when(jnp.logical_and(i >= 1, i <= 4))
        def _():
            z_copy(i).start()

        @pl.when(jnp.logical_or(i == 5, i == 6))
        def _():
            z_half(i).start()

        @pl.when(i == 7)
        def _():
            z_half(5).wait_recv()
            z_half(6).wait_recv()

        @pl.when(jnp.logical_and(i >= 1, i <= 7))
        def _():
            spread(i)

        @pl.when(jnp.logical_and(i >= 1, i <= 8))
        def _():
            s = i - 1
            first, second = p_copies(s)
            on, back = p_halves(s)
            first.wait_recv()
            on.start()
            s_copy(s, 1, p_dn).start()
            second.wait_recv()
            back.start()
            s_copy(s, 2, p_up).start()

        @pl.when(jnp.logical_and(i >= 2, i <= 9))
        def _():
            s = i - 2
            on, back = p_halves(s)
            on.wait_recv()
            back.wait_recv()
            s_copy(s, 3, p_far).start()

        @pl.when(i >= 3)
        def _():
            s = i - 3
            for which in range(4):
                s_copy(s, which, p).wait_recv()
            for copy in out_copies(s):
                copy.start()
            zx, lse, picked = compute(s)
            fresh_row = jnp.concatenate([lse, picked[:, :128] + picked[:, 128:]], axis=1)
            stats_a[me_xy] = jnp.where(planes == zx, fresh_row, stats_a[me_xy])

        return carry

    lax.fori_loop(0, 11, step, 0)

    def a_copy(j):
        return remote(stats_a.at[me_xy], stats_a.at[me_xy], a_s.at[j], a_r.at[me_xy], (j // 4, (j % 4) * 16 + z * 2 + c))

    def a_arrival(j):
        return remote(stats_a.at[j], stats_a.at[j], a_s.at[j], a_r.at[j], (j // 4, (j % 4) * 16 + z * 2 + c))

    def b_copy(j):
        return remote(stats_b.at[me_zc], stats_b.at[me_zc], b_s.at[j], b_r.at[me_zc], (x, y * 16 + j))

    def b_arrival(j):
        return remote(stats_b.at[j], stats_b.at[j], b_s.at[j], b_r.at[j], (x, y * 16 + j))

    def each_other(me, action):
        def one(j, carry):
            @pl.when(j != me)
            def _():
                action(j)
            return carry
        lax.fori_loop(0, 16, one, 0)

    def combine(stats):
        values = [stats[j] for j in range(16)]
        top = values[0]
        for value in values[1:]:
            top = jnp.maximum(top, value)
        total = jnp.exp(values[0] - top)
        added = values[0]
        for value in values[1:]:
            total += jnp.exp(value - top)
            added += value
        return jnp.where(lanes < BLOCK, top + jnp.log(total), added)

    each_other(me_xy, lambda j: a_copy(j).start())
    each_other(me_xy, lambda j: a_arrival(j).wait_recv())
    stats_b[me_zc] = combine(stats_a)
    each_other(me_zc, lambda j: b_copy(j).start())
    each_other(me_zc, lambda j: b_arrival(j).wait_recv())
    final = combine(stats_b)
    signed = jnp.where(lanes < BLOCK, final, -final)
    loss_ref[...] = jnp.sum(jnp.sum(signed, axis=1, keepdims=True), axis=0, keepdims=True) * (1.0 / TOKENS)
    for zx in range(NZ):
        log_norm = final[zx:zx + 1, :BLOCK]
        chosen = (rows == samp_ref[zx:zx + 1, :]).astype(jnp.float32)
        signal_ref[:, zx * BLOCK:(zx + 1) * BLOCK] = (jnp.exp(logits[zx] - log_norm) - chosen).astype(jnp.bfloat16)

    pair_copy.wait_send()
    for copy in q_copies:
        copy.wait_send()
    z_first().wait_send()

    def finish(s, carry):
        @pl.when(s <= 4)
        def _():
            z_copy(s).wait_send()

        for copy in p_copies(s) + p_halves(s):
            copy.wait_send()
        for which in range(4):
            s_copy(s, which, p).wait_send()
        for copy in out_copies(s):
            copy.wait()
        return carry

    lax.fori_loop(0, 8, finish, 0)
    z_half(5).wait_send()
    z_half(6).wait_send()
    each_other(me_xy, lambda j: a_copy(j).wait_send())
    each_other(me_zc, lambda j: b_copy(j).wait_send())


def gather_call(features, head, true_labels, sampled_labels):
    dma = pltpu.SemaphoreType.DMA
    vmem = pl.BlockSpec(memory_space=pltpu.VMEM)
    return pl.pallas_call(
        gather_kernel,
        out_shape=(
            jax.ShapeDtypeStruct((NZ, NX, NY, ROWS, D), jnp.bfloat16),
            jax.ShapeDtypeStruct((VOC, TOKENS), jnp.bfloat16),
            jax.ShapeDtypeStruct((1, 1), jnp.float32),
        ),
        in_specs=[vmem] * 4,
        out_specs=(pl.BlockSpec(memory_space=pl.ANY), vmem, vmem),
        scratch_shapes=[
            pltpu.VMEM((2, 8, HALF), jnp.bfloat16),
            pltpu.VMEM((2, NZ, 4, 4, ROWS, HALF), jnp.bfloat16),
            pltpu.VMEM((NZ, VOC, BLOCK), jnp.float32),
            pltpu.VMEM((16, NZ, STAT), jnp.float32),
            pltpu.VMEM((16, NZ, STAT), jnp.float32),
            dma, dma, dma((3,)), dma((3,)), dma((8,)), dma((8,)), dma((2,)), dma((2,)),
            dma((8, 4)), dma((8, 4)), dma((8, 4)), dma((8, 4)),
            dma((16,)), dma((16,)), dma((16,)), dma((16,)), dma((8, 5)),
        ],
        compiler_params=pltpu.CompilerParams(collective_id=0, has_side_effects=True, vmem_limit_bytes=40 << 20),
        name="gather_logits",
    )(features, head, true_labels, sampled_labels)


def update_kernel(signal_ref, feats_ref, momentum_ref, hessian_ref, fresh_ref, clipped_ref):
    gradient = jnp.dot(signal_ref[...], feats_ref[...], preferred_element_type=jnp.float32)
    fresh = hess_decay * hessian_ref[...].astype(jnp.float32) + (1.0 - hess_decay) * gradient * gradient
    fresh_ref[...] = fresh.astype(jnp.bfloat16)
    clipped = jnp.clip(momentum_ref[...].astype(jnp.float32) / (clip_scale * fresh), -1.0, 1.0)
    clipped_ref[...] = clipped.astype(jnp.bfloat16)


def update_call(signal, feats, momentum, hessian):
    width = 512
    tile = pl.BlockSpec((VOC, width), lambda j: (0, j))
    out = jax.ShapeDtypeStruct((VOC, D), jnp.bfloat16)
    return pl.pallas_call(
        update_kernel,
        grid=(D // width,),
        out_shape=(out, out),
        in_specs=[
            pl.BlockSpec((VOC, TOKENS), lambda j: (0, 0)),
            pl.BlockSpec((TOKENS, width), lambda j: (0, j)),
            tile,
            tile,
        ],
        out_specs=(tile, tile),
        compiler_params=pltpu.CompilerParams(vmem_limit_bytes=40 << 20),
        name="gradient_update",
    )(signal, feats, momentum, hessian)


def by_plane(labels):
    return labels.reshape(NX, NY, NZ, ROWS).transpose(2, 0, 1, 3).reshape(NZ, BLOCK)


def shards(features, head, momentum, hessian, true_labels, sampled_labels):
    feats, signal, loss = gather_call(features, head, by_plane(true_labels), by_plane(sampled_labels))
    fresh, clipped = update_call(signal, feats.reshape(TOKENS, D), momentum, hessian)
    return (loss.reshape(()), fresh, clipped)


def solution(mesh):
    rows = P(("dp", "vocab"), None)
    return jax.shard_map(
        shards,
        mesh=mesh,
        in_specs=(rows, rows, rows, rows, P(), P()),
        out_specs=(P(), rows, rows),
        check_vma=False,
    )
```

```python
import jax
import jax.numpy as jnp
from jax import lax
from jax.experimental import pallas as pl
from jax.experimental.pallas import tpu as pltpu
from jax.sharding import PartitionSpec as P

MESH = pl.DeviceIdType.MESH
hess_decay = 0.99
clip_scale = 0.05

NX, NY, NZ = 4, 4, 8
D = 4096
HALF = D // 2
ROWS = 16
BLOCK = 256
TOKENS = 2048
VOC = 256
STAT = 384
LAG1, LAG2, LAG3 = 2, 4, 5


def permute_labels(raw_ref, true_ref, samp_ref):
    labels = jnp.concatenate([raw_ref[0], raw_ref[1]], axis=0)
    pieces = jnp.concatenate([labels >> 8, labels & 255], axis=0).astype(jnp.float32).astype(jnp.bfloat16)
    source = lax.broadcasted_iota(jnp.int32, (128, BLOCK), 0)
    lane = lax.broadcasted_iota(jnp.int32, (128, BLOCK), 1)
    chip = lax.broadcasted_iota(jnp.int32, (ROWS, BLOCK), 0)
    owner = lax.broadcasted_iota(jnp.int32, (ROWS, BLOCK), 1) >> 4
    for zx in range(NZ):
        pick = (source == zx * ROWS + (lane & 15)).astype(jnp.float32).astype(jnp.bfloat16)
        spread = jnp.dot(pieces, pick, preferred_element_type=jnp.float32)
        rows = [jnp.sum(jnp.where(chip == owner, spread[k * 16:(k + 1) * 16], 0.0), axis=0, keepdims=True) for k in range(4)]
        true_ref[zx:zx + 1, :] = (rows[0] * 256.0 + rows[2]).astype(jnp.int32)
        samp_ref[zx:zx + 1, :] = (rows[1] * 256.0 + rows[3]).astype(jnp.int32)


def gather_kernel(feat_ref, head_hbm, true_hbm, samp_hbm,
                  held, signal_ref, loss_ref,
                  pair, head_ref, raw_ref, true_ref, samp_ref, logits, stats_a, stats_b,
                  pair_s, pair_r, q_s, q_r, zf_s, zf_r, z_s, z_r, zh_s, zh_r,
                  pf_s, pf_r, p_s, p_r, s_s, s_r, a_s, a_r, b_s, b_r, own_sem, head_sem, raw_sem):
    x = lax.axis_index("dp")
    v = lax.axis_index("vocab")
    y, z, c = v // 16, (v // 2) % 8, v % 2
    p = jnp.where(c == 0, x, y)
    q = jnp.where(c == 0, y, x)

    def device(px, qx, zx):
        xx = jnp.where(c == 0, px, qx)
        yy = jnp.where(c == 0, qx, px)
        return (xx, yy * 16 + zx * 2 + c)

    sister = (x, y * 16 + z * 2 + 1 - c)
    p_up, p_dn, p_far = (p + 1) % 4, (p + 3) % 4, (p + 2) % 4
    q_up, q_dn, q_far = (q + 1) % 4, (q + 3) % 4, (q + 2) % 4
    z_up, z_dn = (z + 1) % 8, (z + 7) % 8

    def remote(src, dst, ssem, rsem, dev):
        return pltpu.make_async_remote_copy(src, dst, ssem, rsem, device_id=dev, device_id_type=MESH)

    raw_copies = [pltpu.make_async_copy(true_hbm, raw_ref.at[0], raw_sem.at[0]),
                  pltpu.make_async_copy(samp_hbm, raw_ref.at[1], raw_sem.at[1])]
    for copy in raw_copies:
        copy.start()
    head_copy = pltpu.make_async_copy(head_hbm, head_ref, head_sem)
    head_copy.start()
    own_copy = pltpu.make_async_copy(feat_ref.at[:, pl.ds(pl.multiple_of(c * HALF, HALF), HALF)], pair.at[c], own_sem)
    own_copy.start()
    barrier = pltpu.get_barrier_semaphore()
    for dev in (sister, device(p_up, q, z), device(p_dn, q, z), device(p, q_up, z), device(p, q_dn, z),
                device(p, q, z_up), device(p, q, z_dn)):
        pl.semaphore_signal(barrier, inc=1, device_id=dev, device_id_type=MESH)
    pl.semaphore_wait(barrier, 7)

    theirs = pl.multiple_of((1 - c) * HALF, HALF)
    pair_copy = remote(feat_ref.at[:, pl.ds(theirs, HALF)], pair.at[c], pair_s, pair_r, sister)
    pair_copy.start()
    own_copy.wait()
    pair_copy.wait_recv()
    held[c, z, p, q] = pair[...].reshape(ROWS, HALF)

    def slab(qx):
        return held.at[c, z, p, qx]

    q_copies = [
        remote(slab(q), slab(q), q_s.at[0], q_r.at[0], device(p, q_up, z)),
        remote(slab(q), slab(q), q_s.at[1], q_r.at[1], device(p, q_dn, z)),
        remote(slab(q_dn), slab(q_dn), q_s.at[2], q_r.at[2], device(p, q_up, z)),
    ]
    order = (q, q_dn, q_up, q_far)

    def early(r):
        piece = slab(order[r])
        return [remote(piece, piece, pf_s.at[0, r], pf_r.at[0, r], device(p_up, q, z)),
                remote(piece, piece, pf_s.at[1, r], pf_r.at[1, r], device(p_dn, q, z)),
                remote(piece, piece, zf_s.at[0, r], zf_r.at[0, r], device(p, q, z_up)),
                remote(piece, piece, zf_s.at[1, r], zf_r.at[1, r], device(p, q, z_dn))]

    def start_early(r):
        for copy in early(r):
            copy.start()

    def plane(s):
        off = jnp.where(s % 2 == 1, 8 - (s + 1) // 2, s // 2)
        return (z + off) % 8

    def chunk(zx, px):
        return held.at[c, zx, px]

    def part(zx, px, half):
        return held.at[c, zx, px, pl.ds(half * 2, 2)]

    def z_copy(s):
        zx = plane(s)
        to = jnp.where(s % 2 == 1, z_up, z_dn)
        return remote(chunk(zx, p), chunk(zx, p), z_s.at[s + 2], z_r.at[s + 2], device(p, q, to))

    def z_half(s):
        zx = plane(s)
        to = jnp.where(s % 2 == 1, z_up, z_dn)
        return remote(part(zx, p, s - 5), part(zx, p, s - 5), zh_s.at[s - 5], zh_r.at[s - 5], device(p, q, to))

    def p_copies(s):
        zx = plane(s)
        return (remote(chunk(zx, p), chunk(zx, p), p_s.at[s, 0], p_r.at[s, 0], device(p_up, q, z)),
                remote(chunk(zx, p), chunk(zx, p), p_s.at[s, 1], p_r.at[s, 1], device(p_dn, q, z)))

    def p_halves(s):
        zx = plane(s)
        return (remote(part(zx, p_dn, 0), part(zx, p_dn, 0), p_s.at[s, 2], p_r.at[s, 2], device(p_up, q, z)),
                remote(part(zx, p_up, 1), part(zx, p_up, 1), p_s.at[s, 3], p_r.at[s, 3], device(p_dn, q, z)))

    def s_copy(s, which, px):
        zx = plane(s)
        return remote(chunk(zx, px), chunk(zx, px), s_s.at[s, which], s_r.at[s, which], sister)

    q_copies[0].start()
    q_copies[1].start()
    start_early(0)
    q_copies[0].wait_recv()
    q_copies[2].start()
    start_early(1)
    q_copies[1].wait_recv()
    start_early(2)
    for copy in raw_copies:
        copy.wait()
    permute_labels(raw_ref, true_ref, samp_ref)
    q_copies[2].wait_recv()
    start_early(3)
    s_copy(0, 0, p).start()

    own_offset = (x * 64 + v) * VOC
    rows = own_offset + lax.broadcasted_iota(jnp.int32, (VOC, BLOCK), 0)
    lanes = lax.broadcasted_iota(jnp.int32, (1, STAT), 1)
    planes = lax.broadcasted_iota(jnp.int32, (NZ, STAT), 0)
    me_xy = x * 4 + y
    me_zc = z * 2 + c
    stats_a[me_xy] = jnp.zeros((NZ, STAT), jnp.float32)

    def compute(s):
        zx = plane(s)
        left = held[0, zx].reshape(BLOCK, HALF)
        total = lax.dot_general(head_ref[:, :HALF], left, (((1,), (1,)), ((), ())), preferred_element_type=jnp.float32)
        right = jnp.concatenate([held[1, zx, yy, xx] for xx in range(NX) for yy in range(NY)], axis=0)
        total += lax.dot_general(head_ref[:, HALF:], right, (((1,), (1,)), ((), ())), preferred_element_type=jnp.float32)
        logits[zx] = total
        highest = jnp.max(total, axis=0, keepdims=True)
        lse = highest + jnp.log(jnp.sum(jnp.exp(total - highest), axis=0, keepdims=True))
        labels = true_ref[pl.ds(zx, 1), :]
        picked = jnp.sum(jnp.where(rows == labels, total, 0.0), axis=0, keepdims=True)
        fresh_row = jnp.concatenate([lse, picked[:, :128] + picked[:, 128:]], axis=1)
        stats_a[me_xy] = jnp.where(planes == zx, fresh_row, stats_a[me_xy])

    def step(i, carry):
        @pl.when(jnp.logical_or(i == 1, i == 2))
        def _():
            for r in range(4):
                piece = slab(q)
                remote(piece, piece, zf_s.at[i - 1, r], zf_r.at[i - 1, r], sister).wait_recv()

        @pl.when(jnp.logical_and(i >= 3, i <= 6))
        def _():
            z_copy(i - 2).wait_recv()

        @pl.when(jnp.logical_and(i >= 1, i <= 4))
        def _():
            z_copy(i).start()

        @pl.when(jnp.logical_or(i == 5, i == 6))
        def _():
            z_half(i).start()

        @pl.when(i == 7)
        def _():
            z_half(5).wait_recv()
            z_half(6).wait_recv()

        @pl.when(jnp.logical_and(i >= 1, i <= 7))
        def _():
            for copy in p_copies(i):
                copy.start()
            s_copy(i, 0, p).start()

        @pl.when(jnp.logical_and(i >= LAG1, i <= LAG1 + 7))
        def _():
            s = i - LAG1
            on, back = p_halves(s)

            def arrived(way):
                @pl.when(s == 0)
                def _():
                    for r in range(4):
                        piece = slab(q)
                        remote(piece, piece, pf_s.at[way, r], pf_r.at[way, r], sister).wait_recv()

                @pl.when(s > 0)
                def _():
                    p_copies(s)[way].wait_recv()

            arrived(0)
            on.start()
            s_copy(s, 1, p_dn).start()
            arrived(1)
            back.start()
            s_copy(s, 2, p_up).start()

        @pl.when(jnp.logical_and(i >= LAG2, i <= LAG2 + 7))
        def _():
            s = i - LAG2
            on, back = p_halves(s)
            on.wait_recv()
            back.wait_recv()
            s_copy(s, 3, p_far).start()

        @pl.when(i >= LAG3)
        def _():
            s = i - LAG3
            for which in range(4):
                s_copy(s, which, p).wait_recv()
            compute(s)

        return carry

    head_copy.wait()
    lax.fori_loop(1, 8 + LAG3, step, 0)

    def a_copy(j):
        return remote(stats_a.at[me_xy], stats_a.at[me_xy], a_s.at[j], a_r.at[me_xy], (j // 4, (j % 4) * 16 + z * 2 + c))

    def a_arrival(j):
        return remote(stats_a.at[j], stats_a.at[j], a_s.at[j], a_r.at[j], (j // 4, (j % 4) * 16 + z * 2 + c))

    def b_copy(j):
        return remote(stats_b.at[me_zc], stats_b.at[me_zc], b_s.at[j], b_r.at[me_zc], (x, y * 16 + j))

    def b_arrival(j):
        return remote(stats_b.at[j], stats_b.at[j], b_s.at[j], b_r.at[j], (x, y * 16 + j))

    def each_other(me, action):
        def one(j, carry):
            @pl.when(j != me)
            def _():
                action(j)
            return carry
        lax.fori_loop(0, 16, one, 0)

    def combine(stats):
        values = [stats[j] for j in range(16)]
        top = values[0]
        for value in values[1:]:
            top = jnp.maximum(top, value)
        total = jnp.exp(values[0] - top)
        added = values[0]
        for value in values[1:]:
            total += jnp.exp(value - top)
            added += value
        return jnp.where(lanes < BLOCK, top + jnp.log(total), added)

    each_other(me_xy, lambda j: a_copy(j).start())

    pair_copy.wait_send()
    for copy in q_copies:
        copy.wait_send()
    for r in range(4):
        for copy in early(r):
            copy.wait_send()

    def finish(s, carry):
        @pl.when(jnp.logical_and(s >= 1, s <= 4))
        def _():
            z_copy(s).wait_send()

        @pl.when(s >= 1)
        def _():
            for copy in p_copies(s):
                copy.wait_send()

        for copy in p_halves(s):
            copy.wait_send()
        for which in range(4):
            s_copy(s, which, p).wait_send()
        return carry

    lax.fori_loop(0, 8, finish, 0)
    z_half(5).wait_send()
    z_half(6).wait_send()

    each_other(me_xy, lambda j: a_arrival(j).wait_recv())
    stats_b[me_zc] = combine(stats_a)
    each_other(me_zc, lambda j: b_copy(j).start())
    each_other(me_xy, lambda j: a_copy(j).wait_send())
    each_other(me_zc, lambda j: b_arrival(j).wait_recv())
    final = combine(stats_b)
    signed = jnp.where(lanes < BLOCK, final, -final)
    loss_ref[...] = jnp.sum(jnp.sum(signed, axis=1, keepdims=True), axis=0, keepdims=True) * (1.0 / TOKENS)
    for zx in range(NZ):
        log_norm = final[zx:zx + 1, :BLOCK]
        chosen = (rows == samp_ref[zx:zx + 1, :]).astype(jnp.float32)
        signal_ref[:, zx * BLOCK:(zx + 1) * BLOCK] = (jnp.exp(logits[zx] - log_norm) - chosen).astype(jnp.bfloat16)
    each_other(me_zc, lambda j: b_copy(j).wait_send())


def gather_call(features, head, true_labels, sampled_labels):
    dma = pltpu.SemaphoreType.DMA
    vmem = pl.BlockSpec(memory_space=pltpu.VMEM)
    hbm = pl.BlockSpec(memory_space=pltpu.HBM)
    return pl.pallas_call(
        gather_kernel,
        out_shape=(
            jax.ShapeDtypeStruct((2, NZ, 4, 4, ROWS, HALF), jnp.bfloat16),
            jax.ShapeDtypeStruct((VOC, TOKENS), jnp.bfloat16),
            jax.ShapeDtypeStruct((1, 1), jnp.float32),
        ),
        in_specs=[hbm] * 4,
        out_specs=(vmem, vmem, vmem),
        scratch_shapes=[
            pltpu.VMEM((2, 8, HALF), jnp.bfloat16),
            pltpu.VMEM((VOC, D), jnp.bfloat16),
            pltpu.VMEM((2, 16, 128), jnp.int32),
            pltpu.VMEM((NZ, BLOCK), jnp.int32),
            pltpu.VMEM((NZ, BLOCK), jnp.int32),
            pltpu.VMEM((NZ, VOC, BLOCK), jnp.float32),
            pltpu.VMEM((16, NZ, STAT), jnp.float32),
            pltpu.VMEM((16, NZ, STAT), jnp.float32),
            dma, dma, dma((3,)), dma((3,)), dma((2, 4)), dma((2, 4)), dma((8,)), dma((8,)), dma((2,)), dma((2,)),
            dma((2, 4)), dma((2, 4)), dma((8, 4)), dma((8, 4)), dma((8, 4)), dma((8, 4)),
            dma((16,)), dma((16,)), dma((16,)), dma((16,)), dma, dma, dma((2,)),
        ],
        compiler_params=pltpu.CompilerParams(collective_id=0, has_side_effects=True, vmem_limit_bytes=20 << 20),
        name="gather_logits",
    )(features, head, true_labels, sampled_labels)


def update_kernel(signal_ref, feats_ref, momentum_ref, hessian_ref, fresh_ref, clipped_ref):
    j = pl.program_id(0)
    width = fresh_ref.shape[1]
    steps = HALF // width

    def update(half):
        columns = pl.ds(pl.multiple_of((j - half * steps) * width, width), width)
        if half == 0:
            feats = feats_ref[0, :, :, :, :, columns].reshape(TOKENS, width)
        else:
            feats = jnp.concatenate(
                [feats_ref[1, zz, yy, xx, :, columns] for zz in range(NZ) for xx in range(NX) for yy in range(NY)], axis=0)
        gradient = jnp.dot(signal_ref[...], feats, preferred_element_type=jnp.float32)
        fresh = hess_decay * hessian_ref[...].astype(jnp.float32) + (1.0 - hess_decay) * gradient * gradient
        fresh_ref[...] = fresh.astype(jnp.bfloat16)
        clipped = jnp.clip(momentum_ref[...].astype(jnp.float32) / (clip_scale * fresh), -1.0, 1.0)
        clipped_ref[...] = clipped.astype(jnp.bfloat16)

    pl.when(j < steps)(lambda: update(0))
    pl.when(j >= steps)(lambda: update(1))


def update_call(signal, feats, momentum, hessian):
    width = 1024
    tile = pl.BlockSpec((VOC, width), lambda j: (0, j))
    out = jax.ShapeDtypeStruct((VOC, D), jnp.bfloat16)
    return pl.pallas_call(
        update_kernel,
        grid=(D // width,),
        out_shape=(out, out),
        in_specs=[
            pl.BlockSpec(memory_space=pltpu.VMEM),
            pl.BlockSpec(memory_space=pltpu.VMEM),
            tile,
            tile,
        ],
        out_specs=(tile, tile),
        compiler_params=pltpu.CompilerParams(vmem_limit_bytes=20 << 20),
        name="gradient_update",
    )(signal, feats, momentum, hessian)


def shards(features, head, momentum, hessian, true_labels, sampled_labels):
    features, head, momentum, hessian, true_labels, sampled_labels = (
        pltpu.with_memory_space_constraint(a, pltpu.HBM)
        for a in (features, head, momentum, hessian, true_labels.reshape(16, 128), sampled_labels.reshape(16, 128)))
    feats, signal, loss = gather_call(features, head, true_labels, sampled_labels)
    fresh, clipped = update_call(signal, feats, momentum, hessian)
    return (loss.reshape(()), fresh, clipped)


def solution(mesh):
    rows = P(("dp", "vocab"), None)
    return jax.shard_map(
        shards,
        mesh=mesh,
        in_specs=(rows, rows, rows, rows, P(), P()),
        out_specs=(P(), rows, rows),
        check_vma=False,
    )
```

```python
import jax
import jax.numpy as jnp
from jax import lax
from jax.experimental import pallas as pl
from jax.experimental.pallas import tpu as pltpu
from jax.sharding import PartitionSpec as P

MESH = pl.DeviceIdType.MESH
hess_decay = 0.99
clip_scale = 0.05

NX, NY, NZ = 4, 4, 8
D = 4096
HALF = D // 2
ROWS = 16
BLOCK = 256
TOKENS = 2048
VOC = 256
STAT = 384
LAG1, LAG2, LAG3 = 6, 12, 14


def permute_labels(raw_ref, true_ref, samp_ref):
    labels = jnp.concatenate([raw_ref[0], raw_ref[1]], axis=0)
    pieces = jnp.concatenate([labels >> 8, labels & 255], axis=0).astype(jnp.float32).astype(jnp.bfloat16)
    source = lax.broadcasted_iota(jnp.int32, (128, BLOCK), 0)
    lane = lax.broadcasted_iota(jnp.int32, (128, BLOCK), 1)
    chip = lax.broadcasted_iota(jnp.int32, (ROWS, BLOCK), 0)
    owner = lax.broadcasted_iota(jnp.int32, (ROWS, BLOCK), 1) >> 4
    for zx in range(NZ):
        pick = (source == zx * ROWS + (lane & 15)).astype(jnp.float32).astype(jnp.bfloat16)
        spread = jnp.dot(pieces, pick, preferred_element_type=jnp.float32)
        rows = [jnp.sum(jnp.where(chip == owner, spread[k * 16:(k + 1) * 16], 0.0), axis=0, keepdims=True) for k in range(4)]
        true_ref[zx:zx + 1, :] = (rows[0] * 256.0 + rows[2]).astype(jnp.int32)
        samp_ref[zx:zx + 1, :] = (rows[1] * 256.0 + rows[3]).astype(jnp.int32)


def gather_kernel(feat_ref, head_hbm, momentum_hbm, hessian_hbm, true_hbm, samp_hbm,
                  held, signal_ref, momentum_ref, hessian_ref, loss_ref,
                  pair, head_ref, raw_ref, true_ref, samp_ref, logits, stats_a, stats_b,
                  pair_s, pair_r, q_s, q_r, zf_s, zf_r, z_s, z_r,
                  pf_s, pf_r, p_s, p_r, far_s, far_r, s_s, s_r, a_s, a_r, b_s, b_r, own_sem, head_sem, raw_sem, state_sem):
    x = lax.axis_index("dp")
    v = lax.axis_index("vocab")
    y, z, c = v // 16, (v // 2) % 8, v % 2
    p = jnp.where(c == 0, x, y)
    q = jnp.where(c == 0, y, x)

    def device(px, qx, zx):
        xx = jnp.where(c == 0, px, qx)
        yy = jnp.where(c == 0, qx, px)
        return (xx, yy * 16 + zx * 2 + c)

    sister = (x, y * 16 + z * 2 + 1 - c)
    p_up, p_dn, p_far = (p + 1) % 4, (p + 3) % 4, (p + 2) % 4
    q_up, q_dn, q_far = (q + 1) % 4, (q + 3) % 4, (q + 2) % 4
    z_up, z_dn = (z + 1) % 8, (z + 7) % 8

    def remote(src, dst, ssem, rsem, dev):
        return pltpu.make_async_remote_copy(src, dst, ssem, rsem, device_id=dev, device_id_type=MESH)

    raw_copies = [pltpu.make_async_copy(true_hbm, raw_ref.at[0], raw_sem.at[0]),
                  pltpu.make_async_copy(samp_hbm, raw_ref.at[1], raw_sem.at[1])]
    for copy in raw_copies:
        copy.start()
    head_copy = pltpu.make_async_copy(head_hbm, head_ref, head_sem)
    head_copy.start()
    own_copy = pltpu.make_async_copy(feat_ref.at[:, pl.ds(pl.multiple_of(c * HALF, HALF), HALF)], pair.at[c], own_sem)
    own_copy.start()
    barrier = pltpu.get_barrier_semaphore()
    for dev in (sister, device(p_up, q, z), device(p_dn, q, z), device(p, q_up, z), device(p, q_dn, z), device(p, q_far, z),
                device(p, q, z_up), device(p, q, z_dn)):
        pl.semaphore_signal(barrier, inc=1, device_id=dev, device_id_type=MESH)
    pl.semaphore_wait(barrier, 8)

    theirs = pl.multiple_of((1 - c) * HALF, HALF)
    pair_copy = remote(feat_ref.at[:, pl.ds(theirs, HALF)], pair.at[c], pair_s, pair_r, sister)
    pair_copy.start()
    own_copy.wait()
    pair_copy.wait_recv()
    held[c, z, p, q] = pair[...].reshape(ROWS, HALF)

    def slab(qx):
        return held.at[c, z, p, qx]

    own = slab(q)
    q_copies = [remote(own, own, q_s.at[k], q_r.at[k], device(p, to, z)) for k, to in enumerate((q_up, q_dn, q_far))]
    order = (q, q_dn, q_up, q_far)

    def early(r):
        piece = slab(order[r])
        return [remote(piece, piece, pf_s.at[0, r], pf_r.at[0, r], device(p_up, q, z)),
                remote(piece, piece, pf_s.at[1, r], pf_r.at[1, r], device(p_dn, q, z)),
                remote(piece, piece, zf_s.at[0, r], zf_r.at[0, r], device(p, q, z_up)),
                remote(piece, piece, zf_s.at[1, r], zf_r.at[1, r], device(p, q, z_dn))]

    def start_early(r):
        for copy in early(r):
            copy.start()

    def plane(s):
        off = jnp.where(s % 2 == 1, 8 - (s + 1) // 2, s // 2)
        return (z + off) % 8

    def chunk(zx, px):
        return held.at[c, zx, px]

    def part(zx, px, half):
        return held.at[c, zx, px, pl.ds(half * 2, 2)]

    def z_copy(s, h):
        piece = part(plane(s), p, h)
        to = jnp.where(s % 2 == 1, z_up, z_dn)
        later = jnp.minimum(s + 2, 7)
        return remote(piece, piece, z_s.at[later, h], z_r.at[later, h], device(p, q, to))

    def p_copies(s, h):
        piece = part(plane(s), p, h)
        return (remote(piece, piece, p_s.at[s, 0, h], p_r.at[s, 0, h], device(p_up, q, z)),
                remote(piece, piece, p_s.at[s, 1, h], p_r.at[s, 1, h], device(p_dn, q, z)))

    def far_copy(s, h):
        piece = part(plane(s), jnp.where(h == 0, p_dn, p_up), h)
        return remote(piece, piece, far_s.at[s, h], far_r.at[s, h], device(jnp.where(h == 0, p_up, p_dn), q, z))

    def s_copy(s, which, px):
        piece = chunk(plane(s), px)
        return remote(piece, piece, s_s.at[s, which], s_r.at[s, which], sister)

    for copy in q_copies:
        copy.start()
    start_early(0)
    for r in range(1, 4):
        q_copies[r - 1].wait_recv()
        start_early(r)
    s_copy(0, 0, p).start()
    for copy in raw_copies:
        copy.wait()
    permute_labels(raw_ref, true_ref, samp_ref)

    state_copies = [pltpu.make_async_copy(momentum_hbm, momentum_ref, state_sem.at[0]),
                    pltpu.make_async_copy(hessian_hbm, hessian_ref, state_sem.at[1])]
    for copy in state_copies:
        copy.start()

    own_offset = (x * 64 + v) * VOC
    rows = own_offset + lax.broadcasted_iota(jnp.int32, (VOC, BLOCK), 0)
    lanes = lax.broadcasted_iota(jnp.int32, (1, STAT), 1)
    planes = lax.broadcasted_iota(jnp.int32, (NZ, STAT), 0)
    me_xy = x * 4 + y
    me_zc = z * 2 + c
    stats_a[me_xy] = jnp.zeros((NZ, STAT), jnp.float32)

    def compute(s):
        zx = plane(s)
        left = held[0, zx].reshape(BLOCK, HALF)
        total = lax.dot_general(head_ref[:, :HALF], left, (((1,), (1,)), ((), ())), preferred_element_type=jnp.float32)
        right = jnp.concatenate([held[1, zx, yy, xx] for xx in range(NX) for yy in range(NY)], axis=0)
        total += lax.dot_general(head_ref[:, HALF:], right, (((1,), (1,)), ((), ())), preferred_element_type=jnp.float32)
        logits[zx] = total
        highest = jnp.max(total, axis=0, keepdims=True)
        lse = highest + jnp.log(jnp.sum(jnp.exp(total - highest), axis=0, keepdims=True))
        labels = true_ref[pl.ds(zx, 1), :]
        picked = jnp.sum(jnp.where(rows == labels, total, 0.0), axis=0, keepdims=True)
        fresh_row = jnp.concatenate([lse, picked[:, :128] + picked[:, 128:]], axis=1)
        stats_a[me_xy] = jnp.where(planes == zx, fresh_row, stats_a[me_xy])

    def step(u, carry):
        @pl.when(jnp.logical_and(u >= LAG1, u <= LAG1 + 15))
        def _():
            s, h = (u - LAG1) // 2, (u - LAG1) % 2

            @pl.when(jnp.logical_and(s == 0, h == 0))
            def _():
                for way in range(2):
                    for r in range(4):
                        piece = slab(q)
                        remote(piece, piece, pf_s.at[way, r], pf_r.at[way, r], sister).wait_recv()

            @pl.when(s > 0)
            def _():
                for copy in p_copies(s, h):
                    copy.wait_recv()

            far_copy(s, h).start()

            @pl.when(h == 1)
            def _():
                s_copy(s, 1, p_dn).start()
                s_copy(s, 2, p_up).start()

        @pl.when(u <= 15)
        def _():
            s, h = u // 2, u % 2

            @pl.when(jnp.logical_and(s <= 2, h == 0))
            def _():
                for r in range(4):
                    piece = slab(q)
                    remote(piece, piece, zf_s.at[s - 1, r], zf_r.at[s - 1, r], sister).wait_recv()

            @pl.when(s >= 3)
            def _():
                piece = part(plane(s), p, h)
                remote(piece, piece, z_s.at[s, h], z_r.at[s, h], sister).wait_recv()

            @pl.when(jnp.logical_or(s <= 4, s == 5 + h))
            def _():
                z_copy(s, h).start()

            for copy in p_copies(s, h):
                copy.start()

            @pl.when(h == 1)
            def _():
                s_copy(s, 0, p).start()

        @pl.when(jnp.logical_and(u >= LAG2, u <= LAG2 + 15))
        def _():
            s, h = (u - LAG2) // 2, (u - LAG2) % 2
            far_copy(s, h).wait_recv()

            @pl.when(h == 1)
            def _():
                s_copy(s, 3, p_far).start()

        @pl.when(jnp.logical_and(u >= LAG3, (u - LAG3) % 2 == 1))
        def _():
            s = (u - LAG3) // 2
            for which in range(4):
                s_copy(s, which, p).wait_recv()
            compute(s)

        return carry

    head_copy.wait()
    lax.fori_loop(2, 16 + LAG3, step, 0)

    def a_copy(j):
        return remote(stats_a.at[me_xy], stats_a.at[me_xy], a_s.at[j], a_r.at[me_xy], (j // 4, (j % 4) * 16 + z * 2 + c))

    def a_arrival(j):
        return remote(stats_a.at[j], stats_a.at[j], a_s.at[j], a_r.at[j], (j // 4, (j % 4) * 16 + z * 2 + c))

    def b_copy(j):
        return remote(stats_b.at[me_zc], stats_b.at[me_zc], b_s.at[j], b_r.at[me_zc], (x, y * 16 + j))

    def b_arrival(j):
        return remote(stats_b.at[j], stats_b.at[j], b_s.at[j], b_r.at[j], (x, y * 16 + j))

    def each_other(me, action):
        def one(j, carry):
            @pl.when(j != me)
            def _():
                action(j)
            return carry
        lax.fori_loop(0, 16, one, 0)

    def span(n, k):
        return min(k, n - k)

    xy_order = sorted(((i, k) for i in range(NX) for k in range(NY) if i or k), key=lambda o: -span(NX, o[0]) - span(NY, o[1]))
    zc_order = sorted(((i, k) for i in range(NZ) for k in range(2) if i or k), key=lambda o: -span(NZ, o[0]) * 2 - o[1])

    def combine(stats):
        values = [stats[j] for j in range(16)]
        top = values[0]
        for value in values[1:]:
            top = jnp.maximum(top, value)
        total = jnp.exp(values[0] - top)
        added = values[0]
        for value in values[1:]:
            total += jnp.exp(value - top)
            added += value
        return jnp.where(lanes < BLOCK, top + jnp.log(total), added)

    for dx, dy in xy_order:
        a_copy(((x + dx) % NX) * 4 + (y + dy) % NY).start()

    pair_copy.wait_send()
    for copy in q_copies:
        copy.wait_send()
    for r in range(4):
        for copy in early(r):
            copy.wait_send()

    def finish(s, carry):
        for h in range(2):
            @pl.when(jnp.logical_and(s >= 1, jnp.logical_or(s <= 4, s == 5 + h)))
            def _():
                z_copy(s, h).wait_send()

            @pl.when(s >= 1)
            def _():
                for copy in p_copies(s, h):
                    copy.wait_send()

            far_copy(s, h).wait_send()
        for which in range(4):
            s_copy(s, which, p).wait_send()
        return carry

    lax.fori_loop(0, 8, finish, 0)
    for copy in state_copies:
        copy.wait()

    for dx, dy in reversed(xy_order):
        a_arrival(((x + dx) % NX) * 4 + (y + dy) % NY).wait_recv()
    stats_b[me_zc] = combine(stats_a)
    for dz, dc in zc_order:
        b_copy(((z + dz) % NZ) * 2 + (c + dc) % 2).start()
    each_other(me_xy, lambda j: a_copy(j).wait_send())
    for dz, dc in reversed(zc_order):
        b_arrival(((z + dz) % NZ) * 2 + (c + dc) % 2).wait_recv()
    final = combine(stats_b)
    signed = jnp.where(lanes < BLOCK, final, -final)
    loss_ref[...] = jnp.sum(jnp.sum(signed, axis=1, keepdims=True), axis=0, keepdims=True) * (1.0 / TOKENS)
    for zx in range(NZ):
        log_norm = final[zx:zx + 1, :BLOCK]
        chosen = (rows == samp_ref[zx:zx + 1, :]).astype(jnp.float32)
        signal_ref[:, zx * BLOCK:(zx + 1) * BLOCK] = (jnp.exp(logits[zx] - log_norm) - chosen).astype(jnp.bfloat16)
    each_other(me_zc, lambda j: b_copy(j).wait_send())


def gather_call(features, head, momentum, hessian, true_labels, sampled_labels):
    dma = pltpu.SemaphoreType.DMA
    vmem = pl.BlockSpec(memory_space=pltpu.VMEM)
    hbm = pl.BlockSpec(memory_space=pltpu.HBM)
    return pl.pallas_call(
        gather_kernel,
        out_shape=(
            jax.ShapeDtypeStruct((2, NZ, 4, 4, ROWS, HALF), jnp.bfloat16),
            jax.ShapeDtypeStruct((VOC, TOKENS), jnp.bfloat16),
            jax.ShapeDtypeStruct((VOC, D), jnp.bfloat16),
            jax.ShapeDtypeStruct((VOC, D), jnp.bfloat16),
            jax.ShapeDtypeStruct((1, 1), jnp.float32),
        ),
        in_specs=[hbm] * 6,
        out_specs=(vmem,) * 5,
        scratch_shapes=[
            pltpu.VMEM((2, 8, HALF), jnp.bfloat16),
            pltpu.VMEM((VOC, D), jnp.bfloat16),
            pltpu.VMEM((2, 16, 128), jnp.int32),
            pltpu.VMEM((NZ, BLOCK), jnp.int32),
            pltpu.VMEM((NZ, BLOCK), jnp.int32),
            pltpu.VMEM((NZ, VOC, BLOCK), jnp.float32),
            pltpu.VMEM((16, NZ, STAT), jnp.float32),
            pltpu.VMEM((16, NZ, STAT), jnp.float32),
            dma, dma, dma((3,)), dma((3,)), dma((2, 4)), dma((2, 4)), dma((8, 2)), dma((8, 2)),
            dma((2, 4)), dma((2, 4)), dma((8, 2, 2)), dma((8, 2, 2)), dma((8, 2)), dma((8, 2)), dma((8, 4)), dma((8, 4)),
            dma((16,)), dma((16,)), dma((16,)), dma((16,)), dma, dma, dma((2,)), dma((2,)),
        ],
        compiler_params=pltpu.CompilerParams(collective_id=0, has_side_effects=True, vmem_limit_bytes=20 << 20),
        name="gather_logits",
    )(features, head, momentum, hessian, true_labels, sampled_labels)


def update_kernel(signal_ref, feats_ref, momentum_ref, hessian_ref, fresh_ref, clipped_ref):
    j = pl.program_id(0)
    width = fresh_ref.shape[1]
    steps = HALF // width

    def update(half):
        columns = pl.ds(pl.multiple_of((j - half * steps) * width, width), width)
        whole = pl.ds(pl.multiple_of(j * width, width), width)
        if half == 0:
            feats = feats_ref[0, :, :, :, :, columns].reshape(TOKENS, width)
        else:
            feats = jnp.concatenate(
                [feats_ref[1, zz, yy, xx, :, columns] for zz in range(NZ) for xx in range(NX) for yy in range(NY)], axis=0)
        gradient = jnp.dot(signal_ref[...], feats, preferred_element_type=jnp.float32)
        fresh = hess_decay * hessian_ref[:, whole].astype(jnp.float32) + (1.0 - hess_decay) * gradient * gradient
        fresh_ref[...] = fresh.astype(jnp.bfloat16)
        clipped = jnp.clip(momentum_ref[:, whole].astype(jnp.float32) / (clip_scale * fresh), -1.0, 1.0)
        clipped_ref[...] = clipped.astype(jnp.bfloat16)

    pl.when(j < steps)(lambda: update(0))
    pl.when(j >= steps)(lambda: update(1))


def update_call(signal, feats, momentum, hessian):
    width = 1024
    tile = pl.BlockSpec((VOC, width), lambda j: (0, j))
    out = jax.ShapeDtypeStruct((VOC, D), jnp.bfloat16)
    return pl.pallas_call(
        update_kernel,
        grid=(D // width,),
        out_shape=(out, out),
        in_specs=[
            pl.BlockSpec(memory_space=pltpu.VMEM),
            pl.BlockSpec(memory_space=pltpu.VMEM),
            pl.BlockSpec(memory_space=pltpu.VMEM),
            pl.BlockSpec(memory_space=pltpu.VMEM),
        ],
        out_specs=(tile, tile),
        compiler_params=pltpu.CompilerParams(vmem_limit_bytes=20 << 20),
        name="gradient_update",
    )(signal, feats, momentum, hessian)


def shards(features, head, momentum, hessian, true_labels, sampled_labels):
    features, head, momentum, hessian, true_labels, sampled_labels = (
        pltpu.with_memory_space_constraint(a, pltpu.HBM)
        for a in (features, head, momentum, hessian, true_labels.reshape(16, 128), sampled_labels.reshape(16, 128)))
    feats, signal, momentum, hessian, loss = gather_call(features, head, momentum, hessian, true_labels, sampled_labels)
    fresh, clipped = update_call(signal, feats, momentum, hessian)
    return (loss.reshape(()), fresh, clipped)


def solution(mesh):
    rows = P(("dp", "vocab"), None)
    return jax.shard_map(
        shards,
        mesh=mesh,
        in_specs=(rows, rows, rows, rows, P(), P()),
        out_specs=(P(), rows, rows),
        check_vma=False,
    )
```

```python
import jax
import jax.numpy as jnp
from jax import lax
from jax.experimental import pallas as pl
from jax.experimental.pallas import tpu as pltpu
from jax.sharding import PartitionSpec as P

MESH = pl.DeviceIdType.MESH
hess_decay = 0.99
clip_scale = 0.05

NX, NY, NZ = 4, 4, 8
D = 4096
HALF = D // 2
ROWS = 16
BLOCK = 256
TOKENS = 2048
VOC = 256
LAG1, LAG2, LAG3 = 6, 12, 14


def permute_labels(raw_ref, true_ref, samp_ref):
    labels = jnp.concatenate([raw_ref[0], raw_ref[1]], axis=0)
    pieces = jnp.concatenate([labels >> 8, labels & 255], axis=0).astype(jnp.float32).astype(jnp.bfloat16)
    source = lax.broadcasted_iota(jnp.int32, (128, BLOCK), 0)
    lane = lax.broadcasted_iota(jnp.int32, (128, BLOCK), 1)
    chip = lax.broadcasted_iota(jnp.int32, (ROWS, BLOCK), 0)
    owner = lax.broadcasted_iota(jnp.int32, (ROWS, BLOCK), 1) >> 4
    for zx in range(NZ):
        pick = (source == zx * ROWS + (lane & 15)).astype(jnp.float32).astype(jnp.bfloat16)
        spread = jnp.dot(pieces, pick, preferred_element_type=jnp.float32)
        rows = [jnp.sum(jnp.where(chip == owner, spread[k * 16:(k + 1) * 16], 0.0), axis=0, keepdims=True) for k in range(4)]
        true_ref[zx:zx + 1, :] = (rows[0] * 256.0 + rows[2]).astype(jnp.int32)
        samp_ref[zx:zx + 1, :] = (rows[1] * 256.0 + rows[3]).astype(jnp.int32)


def gather_kernel(feat_ref, head_hbm, momentum_hbm, hessian_hbm, true_hbm, samp_hbm,
                  held, signal_ref, momentum_ref, hessian_ref, loss_ref,
                  pair, head_ref, raw_ref, true_ref, samp_ref, logits, stats_a, stats_b, pick_a, pick_b,
                  pair_s, pair_r, q_s, q_r, zf_s, zf_r, z_s, z_r,
                  pf_s, pf_r, p_s, p_r, far_s, far_r, s_s, s_r, a_s, a_r, b_s, b_r, c_s, c_r, d_s, d_r, own_sem, head_sem, raw_sem, state_sem):
    x = lax.axis_index("dp")
    v = lax.axis_index("vocab")
    y, z, c = v // 16, (v // 2) % 8, v % 2
    p = jnp.where(c == 0, x, y)
    q = jnp.where(c == 0, y, x)

    def device(px, qx, zx):
        xx = jnp.where(c == 0, px, qx)
        yy = jnp.where(c == 0, qx, px)
        return (xx, yy * 16 + zx * 2 + c)

    sister = (x, y * 16 + z * 2 + 1 - c)
    p_up, p_dn, p_far = (p + 1) % 4, (p + 3) % 4, (p + 2) % 4
    q_up, q_dn, q_far = (q + 1) % 4, (q + 3) % 4, (q + 2) % 4
    z_up, z_dn = (z + 1) % 8, (z + 7) % 8

    def remote(src, dst, ssem, rsem, dev):
        return pltpu.make_async_remote_copy(src, dst, ssem, rsem, device_id=dev, device_id_type=MESH)

    raw_copies = [pltpu.make_async_copy(true_hbm, raw_ref.at[0], raw_sem.at[0]),
                  pltpu.make_async_copy(samp_hbm, raw_ref.at[1], raw_sem.at[1])]
    for copy in raw_copies:
        copy.start()
    head_copy = pltpu.make_async_copy(head_hbm, head_ref, head_sem)
    head_copy.start()
    own_copy = pltpu.make_async_copy(feat_ref.at[:, pl.ds(pl.multiple_of(c * HALF, HALF), HALF)], pair.at[c], own_sem)
    own_copy.start()
    barrier = pltpu.get_barrier_semaphore()
    for dev in (sister, device(p_up, q, z), device(p_dn, q, z), device(p, q_up, z), device(p, q_dn, z), device(p, q_far, z),
                device(p, q, z_up), device(p, q, z_dn)):
        pl.semaphore_signal(barrier, inc=1, device_id=dev, device_id_type=MESH)
    pl.semaphore_wait(barrier, 8)

    theirs = pl.multiple_of((1 - c) * HALF, HALF)
    pair_copy = remote(feat_ref.at[:, pl.ds(theirs, HALF)], pair.at[c], pair_s, pair_r, sister)
    pair_copy.start()
    own_copy.wait()
    pair_copy.wait_recv()
    held[c, z, p, q] = pair[...].reshape(ROWS, HALF)

    def slab(qx):
        return held.at[c, z, p, qx]

    own = slab(q)
    q_copies = [remote(own, own, q_s.at[k], q_r.at[k], device(p, to, z)) for k, to in enumerate((q_up, q_dn, q_far))]
    order = (q, q_dn, q_up, q_far)

    def early(r):
        piece = slab(order[r])
        return [remote(piece, piece, pf_s.at[0, r], pf_r.at[0, r], device(p_up, q, z)),
                remote(piece, piece, pf_s.at[1, r], pf_r.at[1, r], device(p_dn, q, z)),
                remote(piece, piece, zf_s.at[0, r], zf_r.at[0, r], device(p, q, z_up)),
                remote(piece, piece, zf_s.at[1, r], zf_r.at[1, r], device(p, q, z_dn))]

    def start_early(r):
        for copy in early(r):
            copy.start()

    def plane(s):
        off = jnp.where(s % 2 == 1, 8 - (s + 1) // 2, s // 2)
        return (z + off) % 8

    def chunk(zx, px):
        return held.at[c, zx, px]

    def part(zx, px, half):
        return held.at[c, zx, px, pl.ds(half * 2, 2)]

    def z_copy(s, h):
        piece = part(plane(s), p, h)
        to = jnp.where(s % 2 == 1, z_up, z_dn)
        later = jnp.minimum(s + 2, 7)
        return remote(piece, piece, z_s.at[later, h], z_r.at[later, h], device(p, q, to))

    def p_copies(s, h):
        piece = part(plane(s), p, h)
        return (remote(piece, piece, p_s.at[s, 0, h], p_r.at[s, 0, h], device(p_up, q, z)),
                remote(piece, piece, p_s.at[s, 1, h], p_r.at[s, 1, h], device(p_dn, q, z)))

    def far_copy(s, h):
        piece = part(plane(s), jnp.where(h == 0, p_dn, p_up), h)
        return remote(piece, piece, far_s.at[s, h], far_r.at[s, h], device(jnp.where(h == 0, p_up, p_dn), q, z))

    def s_copy(s, which, px):
        piece = chunk(plane(s), px)
        return remote(piece, piece, s_s.at[s, which], s_r.at[s, which], sister)

    for copy in q_copies:
        copy.start()
    start_early(0)
    for r in range(1, 4):
        q_copies[r - 1].wait_recv()
        start_early(r)
    s_copy(0, 0, p).start()
    for copy in raw_copies:
        copy.wait()
    permute_labels(raw_ref, true_ref, samp_ref)

    state_copies = [pltpu.make_async_copy(momentum_hbm, momentum_ref, state_sem.at[0]),
                    pltpu.make_async_copy(hessian_hbm, hessian_ref, state_sem.at[1])]
    for copy in state_copies:
        copy.start()

    own_offset = (x * 64 + v) * VOC
    rows = own_offset + lax.broadcasted_iota(jnp.int32, (VOC, BLOCK), 0)
    planes = lax.broadcasted_iota(jnp.int32, (NZ, BLOCK), 0)
    me_xy = x * 4 + y
    me_zc = z * 2 + c
    stats_a[x * 4 + y] = jnp.zeros((NZ, BLOCK), jnp.float32)
    pick_a[x * 4 + y] = jnp.zeros((1, 128), jnp.float32)

    def compute(s):
        zx = plane(s)
        left = held[0, zx].reshape(BLOCK, HALF)
        total = lax.dot_general(head_ref[:, :HALF], left, (((1,), (1,)), ((), ())), preferred_element_type=jnp.float32)
        right = jnp.concatenate([held[1, zx, yy, xx] for xx in range(NX) for yy in range(NY)], axis=0)
        total += lax.dot_general(head_ref[:, HALF:], right, (((1,), (1,)), ((), ())), preferred_element_type=jnp.float32)
        logits[zx] = total
        highest = jnp.max(total, axis=0, keepdims=True)
        lse = highest + jnp.log(jnp.sum(jnp.exp(total - highest), axis=0, keepdims=True))
        labels = true_ref[pl.ds(zx, 1), :]
        picked = jnp.sum(jnp.where(rows == labels, total, 0.0), axis=0, keepdims=True)
        stats_a[me_xy] = jnp.where(planes == zx, lse, stats_a[me_xy])
        pick_a[me_xy] = pick_a[me_xy] + picked[:, :128] + picked[:, 128:]

    def step(u, carry):
        @pl.when(jnp.logical_and(u >= LAG1, u <= LAG1 + 15))
        def _():
            s, h = (u - LAG1) // 2, (u - LAG1) % 2

            @pl.when(jnp.logical_and(s == 0, h == 0))
            def _():
                for way in range(2):
                    for r in range(4):
                        piece = slab(q)
                        remote(piece, piece, pf_s.at[way, r], pf_r.at[way, r], sister).wait_recv()

            @pl.when(s > 0)
            def _():
                for copy in p_copies(s, h):
                    copy.wait_recv()

            far_copy(s, h).start()

            @pl.when(h == 1)
            def _():
                s_copy(s, 1, p_dn).start()
                s_copy(s, 2, p_up).start()

        @pl.when(u <= 15)
        def _():
            s, h = u // 2, u % 2

            @pl.when(jnp.logical_and(s <= 2, h == 0))
            def _():
                for r in range(4):
                    piece = slab(q)
                    remote(piece, piece, zf_s.at[s - 1, r], zf_r.at[s - 1, r], sister).wait_recv()

            @pl.when(s >= 3)
            def _():
                piece = part(plane(s), p, h)
                remote(piece, piece, z_s.at[s, h], z_r.at[s, h], sister).wait_recv()

            @pl.when(jnp.logical_or(s <= 4, s == 5 + h))
            def _():
                z_copy(s, h).start()

            for copy in p_copies(s, h):
                copy.start()

            @pl.when(h == 1)
            def _():
                s_copy(s, 0, p).start()

        @pl.when(jnp.logical_and(u >= LAG2, u <= LAG2 + 15))
        def _():
            s, h = (u - LAG2) // 2, (u - LAG2) % 2
            far_copy(s, h).wait_recv()

            @pl.when(h == 1)
            def _():
                s_copy(s, 3, p_far).start()

        @pl.when(jnp.logical_and(u >= LAG3, (u - LAG3) % 2 == 1))
        def _():
            s = (u - LAG3) // 2
            for which in range(4):
                s_copy(s, which, p).wait_recv()
            compute(s)

        return carry

    head_copy.wait()
    lax.fori_loop(2, 16 + LAG3, step, 0)

    def a_copy(j):
        return remote(stats_a.at[me_xy], stats_a.at[me_xy], a_s.at[j], a_r.at[me_xy], (j // 4, (j % 4) * 16 + z * 2 + c))

    def c_copy(j):
        return remote(pick_a.at[me_xy], pick_a.at[me_xy], c_s.at[j], c_r.at[me_xy], (j // 4, (j % 4) * 16 + z * 2 + c))

    def d_copy(j):
        return remote(pick_b.at[me_zc], pick_b.at[me_zc], d_s.at[j], d_r.at[me_zc], (x, y * 16 + j))

    def c_arrival(j):
        return remote(pick_a.at[j], pick_a.at[j], c_s.at[j], c_r.at[j], (j // 4, (j % 4) * 16 + z * 2 + c))

    def d_arrival(j):
        return remote(pick_b.at[j], pick_b.at[j], d_s.at[j], d_r.at[j], (x, y * 16 + j))

    def a_arrival(j):
        return remote(stats_a.at[j], stats_a.at[j], a_s.at[j], a_r.at[j], (j // 4, (j % 4) * 16 + z * 2 + c))

    def b_copy(j):
        return remote(stats_b.at[me_zc], stats_b.at[me_zc], b_s.at[j], b_r.at[me_zc], (x, y * 16 + j))

    def b_arrival(j):
        return remote(stats_b.at[j], stats_b.at[j], b_s.at[j], b_r.at[j], (x, y * 16 + j))

    def each_other(me, action):
        def one(j, carry):
            @pl.when(j != me)
            def _():
                action(j)
            return carry
        lax.fori_loop(0, 16, one, 0)

    def span(n, k):
        return min(k, n - k)

    xy_order = sorted(((i, k) for i in range(NX) for k in range(NY) if i or k), key=lambda o: -span(NX, o[0]) - span(NY, o[1]))
    zc_order = sorted(((i, k) for i in range(NZ) for k in range(2) if i or k), key=lambda o: -span(NZ, o[0]) * 2 - o[1])

    def combine(stats):
        values = [stats[j] for j in range(16)]
        top = values[0]
        for value in values[1:]:
            top = jnp.maximum(top, value)
        total = jnp.exp(values[0] - top)
        for value in values[1:]:
            total += jnp.exp(value - top)
        return top + jnp.log(total)

    def add(picks):
        total = picks[0]
        for j in range(1, 16):
            total += picks[j]
        return total

    for dx, dy in xy_order:
        a_copy(((x + dx) % NX) * 4 + (y + dy) % NY).start()
    for dx, dy in xy_order:
        c_copy(((x + dx) % NX) * 4 + (y + dy) % NY).start()

    pair_copy.wait_send()
    for copy in q_copies:
        copy.wait_send()
    for r in range(4):
        for copy in early(r):
            copy.wait_send()

    def finish(s, carry):
        for h in range(2):
            @pl.when(jnp.logical_and(s >= 1, jnp.logical_or(s <= 4, s == 5 + h)))
            def _():
                z_copy(s, h).wait_send()

            @pl.when(s >= 1)
            def _():
                for copy in p_copies(s, h):
                    copy.wait_send()

            far_copy(s, h).wait_send()
        for which in range(4):
            s_copy(s, which, p).wait_send()
        return carry

    lax.fori_loop(0, 8, finish, 0)
    for copy in state_copies:
        copy.wait()

    for dx, dy in reversed(xy_order):
        a_arrival(((x + dx) % NX) * 4 + (y + dy) % NY).wait_recv()
    stats_b[me_zc] = combine(stats_a)
    for dz, dc in zc_order:
        b_copy(((z + dz) % NZ) * 2 + (c + dc) % 2).start()
    for dx, dy in reversed(xy_order):
        c_arrival(((x + dx) % NX) * 4 + (y + dy) % NY).wait_recv()
    pick_b[me_zc] = add(pick_a)
    for dz, dc in zc_order:
        d_copy(((z + dz) % NZ) * 2 + (c + dc) % 2).start()
    each_other(me_xy, lambda j: a_copy(j).wait_send())
    for dz, dc in reversed(zc_order):
        b_arrival(((z + dz) % NZ) * 2 + (c + dc) % 2).wait_recv()
    final = combine(stats_b)
    for zx in range(NZ):
        log_norm = final[zx:zx + 1, :BLOCK]
        chosen = (rows == samp_ref[zx:zx + 1, :]).astype(jnp.float32)
        signal_ref[:, zx * BLOCK:(zx + 1) * BLOCK] = (jnp.exp(logits[zx] - log_norm) - chosen).astype(jnp.bfloat16)
    for dz, dc in reversed(zc_order):
        d_arrival(((z + dz) % NZ) * 2 + (c + dc) % 2).wait_recv()
    spent = jnp.sum(jnp.sum(final, axis=1, keepdims=True), axis=0, keepdims=True)
    loss_ref[...] = (spent - jnp.sum(add(pick_b), axis=1, keepdims=True)) * (1.0 / TOKENS)
    each_other(me_zc, lambda j: b_copy(j).wait_send())
    each_other(me_xy, lambda j: c_copy(j).wait_send())
    each_other(me_zc, lambda j: d_copy(j).wait_send())


def gather_call(features, head, momentum, hessian, true_labels, sampled_labels):
    dma = pltpu.SemaphoreType.DMA
    vmem = pl.BlockSpec(memory_space=pltpu.VMEM)
    hbm = pl.BlockSpec(memory_space=pltpu.HBM)
    return pl.pallas_call(
        gather_kernel,
        out_shape=(
            jax.ShapeDtypeStruct((2, NZ, 4, 4, ROWS, HALF), jnp.bfloat16),
            jax.ShapeDtypeStruct((VOC, TOKENS), jnp.bfloat16),
            jax.ShapeDtypeStruct((VOC, D), jnp.bfloat16),
            jax.ShapeDtypeStruct((VOC, D), jnp.bfloat16),
            jax.ShapeDtypeStruct((1, 1), jnp.float32),
        ),
        in_specs=[hbm] * 6,
        out_specs=(vmem,) * 5,
        scratch_shapes=[
            pltpu.VMEM((2, 8, HALF), jnp.bfloat16),
            pltpu.VMEM((VOC, D), jnp.bfloat16),
            pltpu.VMEM((2, 16, 128), jnp.int32),
            pltpu.VMEM((NZ, BLOCK), jnp.int32),
            pltpu.VMEM((NZ, BLOCK), jnp.int32),
            pltpu.VMEM((NZ, VOC, BLOCK), jnp.float32),
            pltpu.VMEM((16, NZ, BLOCK), jnp.float32),
            pltpu.VMEM((16, NZ, BLOCK), jnp.float32),
            pltpu.VMEM((16, 1, 128), jnp.float32),
            pltpu.VMEM((16, 1, 128), jnp.float32),
            dma, dma, dma((3,)), dma((3,)), dma((2, 4)), dma((2, 4)), dma((8, 2)), dma((8, 2)),
            dma((2, 4)), dma((2, 4)), dma((8, 2, 2)), dma((8, 2, 2)), dma((8, 2)), dma((8, 2)), dma((8, 4)), dma((8, 4)),
            *[dma((16,))] * 8, dma, dma, dma((2,)), dma((2,)),
        ],
        compiler_params=pltpu.CompilerParams(collective_id=0, has_side_effects=True, vmem_limit_bytes=20 << 20),
        name="gather_logits",
    )(features, head, momentum, hessian, true_labels, sampled_labels)


def update_kernel(signal_ref, feats_ref, momentum_ref, hessian_ref, fresh_ref, clipped_ref):
    j = pl.program_id(0)
    width = fresh_ref.shape[1]
    steps = HALF // width

    def update(half):
        columns = pl.ds(pl.multiple_of((j - half * steps) * width, width), width)
        whole = pl.ds(pl.multiple_of(j * width, width), width)
        if half == 0:
            feats = feats_ref[0, :, :, :, :, columns].reshape(TOKENS, width)
        else:
            feats = jnp.concatenate(
                [feats_ref[1, zz, yy, xx, :, columns] for zz in range(NZ) for xx in range(NX) for yy in range(NY)], axis=0)
        gradient = jnp.dot(signal_ref[...], feats, preferred_element_type=jnp.float32)
        fresh = hess_decay * hessian_ref[:, whole].astype(jnp.float32) + (1.0 - hess_decay) * gradient * gradient
        fresh_ref[...] = fresh.astype(jnp.bfloat16)
        clipped = jnp.clip(momentum_ref[:, whole].astype(jnp.float32) / (clip_scale * fresh), -1.0, 1.0)
        clipped_ref[...] = clipped.astype(jnp.bfloat16)

    pl.when(j < steps)(lambda: update(0))
    pl.when(j >= steps)(lambda: update(1))


def update_call(signal, feats, momentum, hessian):
    width = 1024
    tile = pl.BlockSpec((VOC, width), lambda j: (0, j))
    out = jax.ShapeDtypeStruct((VOC, D), jnp.bfloat16)
    return pl.pallas_call(
        update_kernel,
        grid=(D // width,),
        out_shape=(out, out),
        in_specs=[
            pl.BlockSpec(memory_space=pltpu.VMEM),
            pl.BlockSpec(memory_space=pltpu.VMEM),
            pl.BlockSpec(memory_space=pltpu.VMEM),
            pl.BlockSpec(memory_space=pltpu.VMEM),
        ],
        out_specs=(tile, tile),
        compiler_params=pltpu.CompilerParams(vmem_limit_bytes=20 << 20),
        name="gradient_update",
    )(signal, feats, momentum, hessian)


def shards(features, head, momentum, hessian, true_labels, sampled_labels):
    features, head, momentum, hessian, true_labels, sampled_labels = (
        pltpu.with_memory_space_constraint(a, pltpu.HBM)
        for a in (features, head, momentum, hessian, true_labels.reshape(16, 128), sampled_labels.reshape(16, 128)))
    feats, signal, momentum, hessian, loss = gather_call(features, head, momentum, hessian, true_labels, sampled_labels)
    fresh, clipped = update_call(signal, feats, momentum, hessian)
    return (loss.reshape(()), fresh, clipped)


def solution(mesh):
    rows = P(("dp", "vocab"), None)
    return jax.shard_map(
        shards,
        mesh=mesh,
        in_specs=(rows, rows, rows, rows, P(), P()),
        out_specs=(P(), rows, rows),
        check_vma=False,
    )
```

```python
import jax
import jax.numpy as jnp
from jax import lax
from jax.experimental import pallas as pl
from jax.experimental.pallas import tpu as pltpu
from jax.sharding import PartitionSpec as P

MESH = pl.DeviceIdType.MESH
hess_decay = 0.99
clip_scale = 0.05

NX, NY, NZ = 4, 4, 8
D = 4096
HALF = D // 2
ROWS = 16
BLOCK = 256
TOKENS = 2048
VOC = 256
LAG1, LAG2, LAG3 = 6, 12, 14


def permute_labels(raw_ref, true_ref, samp_ref):
    labels = jnp.concatenate([raw_ref[0], raw_ref[1]], axis=0)
    pieces = jnp.concatenate([labels >> 8, labels & 255], axis=0).astype(jnp.float32).astype(jnp.bfloat16)
    source = lax.broadcasted_iota(jnp.int32, (128, BLOCK), 0)
    lane = lax.broadcasted_iota(jnp.int32, (128, BLOCK), 1)
    chip = lax.broadcasted_iota(jnp.int32, (ROWS, BLOCK), 0)
    owner = lax.broadcasted_iota(jnp.int32, (ROWS, BLOCK), 1) >> 4
    for zx in range(NZ):
        pick = (source == zx * ROWS + (lane & 15)).astype(jnp.float32).astype(jnp.bfloat16)
        spread = jnp.dot(pieces, pick, preferred_element_type=jnp.float32)
        rows = [jnp.sum(jnp.where(chip == owner, spread[k * 16:(k + 1) * 16], 0.0), axis=0, keepdims=True) for k in range(4)]
        true_ref[zx:zx + 1, :] = (rows[0] * 256.0 + rows[2]).astype(jnp.int32)
        samp_ref[zx:zx + 1, :] = (rows[1] * 256.0 + rows[3]).astype(jnp.int32)


def gather_kernel(feat_ref, head_hbm, momentum_hbm, hessian_hbm, true_hbm, samp_hbm,
                  held, signal_ref, momentum_ref, hessian_ref, loss_ref,
                  pair, head_ref, raw_ref, true_ref, samp_ref, logits, stats_a, stats_b, pick_a, pick_b,
                  pair_s, pair_r, q_s, q_r, zf_s, zf_r, z_s, z_r,
                  pf_s, pf_r, p_s, p_r, far_s, far_r, s_s, s_r, a_s, a_r, b_s, b_r, c_s, c_r, d_s, d_r, own_sem, head_sem, raw_sem, state_sem):
    x = lax.axis_index("dp")
    v = lax.axis_index("vocab")
    y, z, c = v // 16, (v // 2) % 8, v % 2
    p = jnp.where(c == 0, x, y)
    q = jnp.where(c == 0, y, x)

    def device(px, qx, zx):
        xx = jnp.where(c == 0, px, qx)
        yy = jnp.where(c == 0, qx, px)
        return (xx, yy * 16 + zx * 2 + c)

    sister = (x, y * 16 + z * 2 + 1 - c)
    p_up, p_dn, p_far = (p + 1) % 4, (p + 3) % 4, (p + 2) % 4
    q_up, q_dn, q_far = (q + 1) % 4, (q + 3) % 4, (q + 2) % 4
    z_up, z_dn = (z + 1) % 8, (z + 7) % 8

    def remote(src, dst, ssem, rsem, dev):
        return pltpu.make_async_remote_copy(src, dst, ssem, rsem, device_id=dev, device_id_type=MESH)

    raw_copies = [pltpu.make_async_copy(true_hbm, raw_ref.at[0], raw_sem.at[0]),
                  pltpu.make_async_copy(samp_hbm, raw_ref.at[1], raw_sem.at[1])]
    for copy in raw_copies:
        copy.start()
    head_copy = pltpu.make_async_copy(head_hbm, head_ref, head_sem)
    head_copy.start()
    own_copy = pltpu.make_async_copy(feat_ref.at[:, pl.ds(pl.multiple_of(c * HALF, HALF), HALF)], pair.at[c], own_sem)
    own_copy.start()
    barrier = pltpu.get_barrier_semaphore()
    for dev in (sister, device(p_up, q, z), device(p_dn, q, z), device(p, q_up, z), device(p, q_dn, z), device(p, q_far, z),
                device(p, q, z_up), device(p, q, z_dn)):
        pl.semaphore_signal(barrier, inc=1, device_id=dev, device_id_type=MESH)
    pl.semaphore_wait(barrier, 8)

    theirs = pl.multiple_of((1 - c) * HALF, HALF)
    pair_copy = remote(feat_ref.at[:, pl.ds(theirs, HALF)], pair.at[c], pair_s, pair_r, sister)
    pair_copy.start()
    own_copy.wait()
    pair_copy.wait_recv()
    held[c, z, p, q] = pair[...].reshape(ROWS, HALF)

    def slab(qx):
        return held.at[c, z, p, qx]

    own = slab(q)
    q_copies = [remote(own, own, q_s.at[k], q_r.at[k], device(p, to, z)) for k, to in enumerate((q_up, q_dn, q_far))]
    order = (q, q_dn, q_up, q_far)

    def early(r):
        piece = slab(order[r])
        return [remote(piece, piece, pf_s.at[0, r], pf_r.at[0, r], device(p_up, q, z)),
                remote(piece, piece, pf_s.at[1, r], pf_r.at[1, r], device(p_dn, q, z)),
                remote(piece, piece, zf_s.at[0, r], zf_r.at[0, r], device(p, q, z_up)),
                remote(piece, piece, zf_s.at[1, r], zf_r.at[1, r], device(p, q, z_dn))]

    def start_early(r):
        for copy in early(r):
            copy.start()

    def plane(s):
        off = jnp.where(s % 2 == 1, 8 - (s + 1) // 2, s // 2)
        return (z + off) % 8

    def chunk(zx, px):
        return held.at[c, zx, px]

    def part(zx, px, half):
        return held.at[c, zx, px, pl.ds(half * 2, 2)]

    def z_copy(s, h):
        piece = part(plane(s), p, h)
        to = jnp.where(s % 2 == 1, z_up, z_dn)
        later = jnp.minimum(s + 2, 7)
        return remote(piece, piece, z_s.at[later, h], z_r.at[later, h], device(p, q, to))

    def p_copies(s, h):
        piece = part(plane(s), p, h)
        return (remote(piece, piece, p_s.at[s, 0, h], p_r.at[s, 0, h], device(p_up, q, z)),
                remote(piece, piece, p_s.at[s, 1, h], p_r.at[s, 1, h], device(p_dn, q, z)))

    def far_copy(s, h):
        piece = part(plane(s), jnp.where(h == 0, p_dn, p_up), h)
        return remote(piece, piece, far_s.at[s, h], far_r.at[s, h], device(jnp.where(h == 0, p_up, p_dn), q, z))

    def s_copy(s, which, px):
        piece = chunk(plane(s), px)
        return remote(piece, piece, s_s.at[s, which], s_r.at[s, which], sister)

    for copy in q_copies:
        copy.start()
    start_early(0)
    for r in range(1, 4):
        q_copies[r - 1].wait_recv()
        start_early(r)
    s_copy(0, 0, p).start()
    for copy in raw_copies:
        copy.wait()
    permute_labels(raw_ref, true_ref, samp_ref)

    state_copies = [pltpu.make_async_copy(momentum_hbm, momentum_ref, state_sem.at[0]),
                    pltpu.make_async_copy(hessian_hbm, hessian_ref, state_sem.at[1])]
    for copy in state_copies:
        copy.start()

    own_offset = (x * 64 + v) * VOC
    rows = own_offset + lax.broadcasted_iota(jnp.int32, (VOC, BLOCK), 0)
    planes = lax.broadcasted_iota(jnp.int32, (NZ, BLOCK), 0)
    me_xy = x * 4 + y
    me_zc = z * 2 + c
    stats_a[x * 4 + y] = jnp.zeros((NZ, BLOCK), jnp.float32)
    pick_a[x * 4 + y] = jnp.zeros((1, 128), jnp.float32)

    def compute(s):
        zx = plane(s)
        left = held[0, zx].reshape(BLOCK, HALF)
        total = lax.dot_general(head_ref[:, :HALF], left, (((1,), (1,)), ((), ())), preferred_element_type=jnp.float32)
        right = jnp.concatenate([held[1, zx, yy, xx] for xx in range(NX) for yy in range(NY)], axis=0)
        total += lax.dot_general(head_ref[:, HALF:], right, (((1,), (1,)), ((), ())), preferred_element_type=jnp.float32)
        logits[zx] = total
        highest = jnp.max(total, axis=0, keepdims=True)
        lse = highest + jnp.log(jnp.sum(jnp.exp(total - highest), axis=0, keepdims=True))
        labels = true_ref[pl.ds(zx, 1), :]
        picked = jnp.sum(jnp.where(rows == labels, total, 0.0), axis=0, keepdims=True)
        stats_a[me_xy] = jnp.where(planes == zx, lse, stats_a[me_xy])
        pick_a[me_xy] = pick_a[me_xy] + picked[:, :128] + picked[:, 128:]

    def step(u, carry):
        @pl.when(jnp.logical_and(u >= LAG1, u <= LAG1 + 15))
        def _():
            s, h = (u - LAG1) // 2, (u - LAG1) % 2

            @pl.when(jnp.logical_and(s == 0, h == 0))
            def _():
                for way in range(2):
                    for r in range(4):
                        piece = slab(q)
                        remote(piece, piece, pf_s.at[way, r], pf_r.at[way, r], sister).wait_recv()

            @pl.when(s > 0)
            def _():
                for copy in p_copies(s, h):
                    copy.wait_recv()

            far_copy(s, h).start()

            @pl.when(h == 1)
            def _():
                s_copy(s, 1, p_dn).start()
                s_copy(s, 2, p_up).start()

        @pl.when(u <= 15)
        def _():
            s, h = u // 2, u % 2

            @pl.when(jnp.logical_and(s <= 2, h == 0))
            def _():
                for r in range(4):
                    piece = slab(q)
                    remote(piece, piece, zf_s.at[s - 1, r], zf_r.at[s - 1, r], sister).wait_recv()

            @pl.when(s >= 3)
            def _():
                piece = part(plane(s), p, h)
                remote(piece, piece, z_s.at[s, h], z_r.at[s, h], sister).wait_recv()

            @pl.when(jnp.logical_or(s <= 4, s == 5 + h))
            def _():
                z_copy(s, h).start()

            for copy in p_copies(s, h):
                copy.start()

            @pl.when(h == 1)
            def _():
                s_copy(s, 0, p).start()

        @pl.when(jnp.logical_and(u >= LAG2, u <= LAG2 + 15))
        def _():
            s, h = (u - LAG2) // 2, (u - LAG2) % 2
            far_copy(s, h).wait_recv()

            @pl.when(h == 1)
            def _():
                s_copy(s, 3, p_far).start()

        @pl.when(jnp.logical_and(u >= LAG3, (u - LAG3) % 2 == 1))
        def _():
            s = (u - LAG3) // 2
            for which in range(4):
                s_copy(s, which, p).wait_recv()
            compute(s)

        return carry

    head_copy.wait()
    lax.fori_loop(2, 16 + LAG3, step, 0)

    def a_copy(j):
        return remote(stats_a.at[me_xy], stats_a.at[me_xy], a_s.at[j], a_r.at[me_xy], (j // 4, (j % 4) * 16 + z * 2 + c))

    def c_copy(j):
        return remote(pick_a.at[me_xy], pick_a.at[me_xy], c_s.at[j], c_r.at[me_xy], (j // 4, (j % 4) * 16 + z * 2 + c))

    def d_copy(j):
        return remote(pick_b.at[me_zc], pick_b.at[me_zc], d_s.at[j], d_r.at[me_zc], (x, y * 16 + j))

    def c_arrival(j):
        return remote(pick_a.at[j], pick_a.at[j], c_s.at[j], c_r.at[j], (j // 4, (j % 4) * 16 + z * 2 + c))

    def d_arrival(j):
        return remote(pick_b.at[j], pick_b.at[j], d_s.at[j], d_r.at[j], (x, y * 16 + j))

    def a_arrival(j):
        return remote(stats_a.at[j], stats_a.at[j], a_s.at[j], a_r.at[j], (j // 4, (j % 4) * 16 + z * 2 + c))

    def b_copy(j):
        return remote(stats_b.at[me_zc], stats_b.at[me_zc], b_s.at[j], b_r.at[me_zc], (x, y * 16 + j))

    def b_arrival(j):
        return remote(stats_b.at[j], stats_b.at[j], b_s.at[j], b_r.at[j], (x, y * 16 + j))

    def each_other(me, action):
        def one(j, carry):
            @pl.when(j != me)
            def _():
                action(j)
            return carry
        lax.fori_loop(0, 16, one, 0)

    def span(n, k):
        return min(k, n - k)

    xy_order = sorted(((i, k) for i in range(NX) for k in range(NY) if i or k), key=lambda o: -span(NX, o[0]) - span(NY, o[1]))
    zc_order = sorted(((i, k) for i in range(NZ) for k in range(2) if i or k), key=lambda o: -span(NZ, o[0]) * 2 - o[1])

    def combine(stats):
        values = [stats[j] for j in range(16)]
        top = values[0]
        for value in values[1:]:
            top = jnp.maximum(top, value)
        total = jnp.exp(values[0] - top)
        for value in values[1:]:
            total += jnp.exp(value - top)
        return top + jnp.log(total)

    def add(picks):
        total = picks[0]
        for j in range(1, 16):
            total += picks[j]
        return total

    for dx, dy in xy_order:
        a_copy(((x + dx) % NX) * 4 + (y + dy) % NY).start()
    for dx, dy in xy_order:
        c_copy(((x + dx) % NX) * 4 + (y + dy) % NY).start()

    pair_copy.wait_send()
    for copy in q_copies:
        copy.wait_send()
    for r in range(4):
        for copy in early(r):
            copy.wait_send()

    def finish(s, carry):
        for h in range(2):
            @pl.when(jnp.logical_and(s >= 1, jnp.logical_or(s <= 4, s == 5 + h)))
            def _():
                z_copy(s, h).wait_send()

            @pl.when(s >= 1)
            def _():
                for copy in p_copies(s, h):
                    copy.wait_send()

            far_copy(s, h).wait_send()
        for which in range(4):
            s_copy(s, which, p).wait_send()
        return carry

    lax.fori_loop(0, 8, finish, 0)
    for copy in state_copies:
        copy.wait()

    for dx, dy in reversed(xy_order):
        a_arrival(((x + dx) % NX) * 4 + (y + dy) % NY).wait_recv()
    stats_b[me_zc] = combine(stats_a)
    for dz, dc in zc_order:
        b_copy(((z + dz) % NZ) * 2 + (c + dc) % 2).start()
    for dx, dy in reversed(xy_order):
        c_arrival(((x + dx) % NX) * 4 + (y + dy) % NY).wait_recv()
    pick_b[me_zc] = add(pick_a)
    for dz, dc in zc_order:
        d_copy(((z + dz) % NZ) * 2 + (c + dc) % 2).start()
    each_other(me_xy, lambda j: a_copy(j).wait_send())
    for dz, dc in reversed(zc_order):
        b_arrival(((z + dz) % NZ) * 2 + (c + dc) % 2).wait_recv()
    final = combine(stats_b)
    for zx in range(NZ):
        log_norm = final[zx:zx + 1, :BLOCK]
        chosen = (rows == samp_ref[zx:zx + 1, :]).astype(jnp.float32)
        signal_ref[:, zx * BLOCK:(zx + 1) * BLOCK] = (jnp.exp(logits[zx] - log_norm) - chosen).astype(jnp.bfloat16)
    for dz, dc in reversed(zc_order):
        d_arrival(((z + dz) % NZ) * 2 + (c + dc) % 2).wait_recv()
    spent = jnp.sum(jnp.sum(final, axis=1, keepdims=True), axis=0, keepdims=True)
    loss_ref[...] = (spent - jnp.sum(add(pick_b), axis=1, keepdims=True)) * (1.0 / TOKENS)
    each_other(me_zc, lambda j: b_copy(j).wait_send())
    each_other(me_xy, lambda j: c_copy(j).wait_send())
    each_other(me_zc, lambda j: d_copy(j).wait_send())


def gather_call(features, head, momentum, hessian, true_labels, sampled_labels):
    dma = pltpu.SemaphoreType.DMA
    vmem = pl.BlockSpec(memory_space=pltpu.VMEM)
    hbm = pl.BlockSpec(memory_space=pltpu.HBM)
    return pl.pallas_call(
        gather_kernel,
        out_shape=(
            jax.ShapeDtypeStruct((2, NZ, 4, 4, ROWS, HALF), jnp.bfloat16),
            jax.ShapeDtypeStruct((VOC, TOKENS), jnp.bfloat16),
            jax.ShapeDtypeStruct((VOC, D), jnp.bfloat16),
            jax.ShapeDtypeStruct((VOC, D), jnp.bfloat16),
            jax.ShapeDtypeStruct((1, 1), jnp.float32),
        ),
        in_specs=[hbm] * 6,
        out_specs=(vmem,) * 5,
        scratch_shapes=[
            pltpu.VMEM((2, 8, HALF), jnp.bfloat16),
            pltpu.VMEM((VOC, D), jnp.bfloat16),
            pltpu.VMEM((2, 16, 128), jnp.int32),
            pltpu.VMEM((NZ, BLOCK), jnp.int32),
            pltpu.VMEM((NZ, BLOCK), jnp.int32),
            pltpu.VMEM((NZ, VOC, BLOCK), jnp.float32),
            pltpu.VMEM((16, NZ, BLOCK), jnp.float32),
            pltpu.VMEM((16, NZ, BLOCK), jnp.float32),
            pltpu.VMEM((16, 1, 128), jnp.float32),
            pltpu.VMEM((16, 1, 128), jnp.float32),
            dma, dma, dma((3,)), dma((3,)), dma((2, 4)), dma((2, 4)), dma((8, 2)), dma((8, 2)),
            dma((2, 4)), dma((2, 4)), dma((8, 2, 2)), dma((8, 2, 2)), dma((8, 2)), dma((8, 2)), dma((8, 4)), dma((8, 4)),
            *[dma((16,))] * 8, dma, dma, dma((2,)), dma((2,)),
        ],
        compiler_params=pltpu.CompilerParams(collective_id=0, has_side_effects=True, vmem_limit_bytes=20 << 20),
        name="gather_logits",
    )(features, head, momentum, hessian, true_labels, sampled_labels)


def update_kernel(signal_ref, feats_ref, momentum_ref, hessian_ref, fresh_ref, clipped_ref):
    j = pl.program_id(0)
    width = fresh_ref.shape[1]
    steps = HALF // width

    def update(half):
        columns = pl.ds(pl.multiple_of((j - half * steps) * width, width), width)
        whole = pl.ds(pl.multiple_of(j * width, width), width)
        if half == 0:
            feats = feats_ref[0, :, :, :, :, columns].reshape(TOKENS, width)
        else:
            feats = jnp.concatenate(
                [feats_ref[1, zz, yy, xx, :, columns] for zz in range(NZ) for xx in range(NX) for yy in range(NY)], axis=0)
        gradient = jnp.dot(signal_ref[...], feats, preferred_element_type=jnp.float32)
        fresh = hess_decay * hessian_ref[:, whole].astype(jnp.float32) + (1.0 - hess_decay) * gradient * gradient
        fresh_ref[...] = fresh.astype(jnp.bfloat16)
        clipped = jnp.clip(momentum_ref[:, whole].astype(jnp.float32) / (clip_scale * fresh), -1.0, 1.0)
        clipped_ref[...] = clipped.astype(jnp.bfloat16)

    pl.when(j < steps)(lambda: update(0))
    pl.when(j >= steps)(lambda: update(1))


def update_call(signal, feats, momentum, hessian):
    width = 2048
    tile = pl.BlockSpec((VOC, width), lambda j: (0, j))
    out = jax.ShapeDtypeStruct((VOC, D), jnp.bfloat16)
    return pl.pallas_call(
        update_kernel,
        grid=(D // width,),
        out_shape=(out, out),
        in_specs=[
            pl.BlockSpec(memory_space=pltpu.VMEM),
            pl.BlockSpec(memory_space=pltpu.VMEM),
            pl.BlockSpec(memory_space=pltpu.VMEM),
            pl.BlockSpec(memory_space=pltpu.VMEM),
        ],
        out_specs=(tile, tile),
        compiler_params=pltpu.CompilerParams(vmem_limit_bytes=20 << 20),
        name="gradient_update",
    )(signal, feats, momentum, hessian)


def shards(features, head, momentum, hessian, true_labels, sampled_labels):
    features, head, momentum, hessian, true_labels, sampled_labels = (
        pltpu.with_memory_space_constraint(a, pltpu.HBM)
        for a in (features, head, momentum, hessian, true_labels.reshape(16, 128), sampled_labels.reshape(16, 128)))
    feats, signal, momentum, hessian, loss = gather_call(features, head, momentum, hessian, true_labels, sampled_labels)
    fresh, clipped = update_call(signal, feats, momentum, hessian)
    return (loss.reshape(()), fresh, clipped)


def solution(mesh):
    rows = P(("dp", "vocab"), None)
    return jax.shard_map(
        shards,
        mesh=mesh,
        in_specs=(rows, rows, rows, rows, P(), P()),
        out_specs=(P(), rows, rows),
        check_vma=False,
    )
```
